32 devices in a mesh: stream: 2 (over core), batch: 16 (over z, y, x).
Axes of the slice: x: 2, y: 2, z: 4, core: 2. Of those that a mesh axis runs over, the one named last changes fastest.
Arguments:
- tokens: bfloat16 [2, 8192, 768], P('stream', 'batch'), may hold values from -6 to 6
- seg_ids: int32 [2, 16, 512], P('stream', 'batch'), may hold values from 0 to 3, never falling along the last dimension, each value on 1 to 384 neighbouring positions
- pos_ids: int32 [64], replicated, may hold values from 0 to 63, each once
- q_weight: bfloat16 [768, 768], replicated, may hold values from -0.21875 to 0.21875
- q_bias: bfloat16 [768], replicated, may hold values from -1.796875 to 1.796875
- k_weight: bfloat16 [768, 768], replicated, may hold values from -0.21875 to 0.21875
- v_weight: bfloat16 [768, 768], replicated, may hold values from -0.21875 to 0.21875
- v_bias: bfloat16 [768], replicated, may hold values from -1.796875 to 1.796875
- o_weight: bfloat16 [768, 768], replicated, may hold values from -0.875 to 0.875
- o_bias: bfloat16 [768], replicated, may hold values from -1.796875 to 1.796875
- norm1_gain: bfloat16 [768], replicated, may hold values from 0.5 to 1.5
- norm1_bias: bfloat16 [768], replicated, may hold values from -1.796875 to 1.796875
- up_weight: bfloat16 [768, 3072], replicated, may hold values from -0.21875 to 0.21875
- up_bias: bfloat16 [3072], replicated, may hold values from -1.796875 to 1.796875
- down_weight: bfloat16 [3072, 768], replicated, may hold values from -0.109375 to 0.109375
- down_bias: bfloat16 [768], replicated, may hold values from -1.796875 to 1.796875
- norm2_gain: bfloat16 [768], replicated, may hold values from 0.5 to 1.5
- norm2_bias: bfloat16 [768], replicated, may hold values from -1.1953125 to 1.1953125
Outputs:
- loss: float32 [], replicated
- hidden_out: bfloat16 [2, 8192, 768], P('stream', 'batch')
- grad_input: float32 [2, 8192, 768], P('stream', 'batch')
- grad_q_weight: float32 [768, 768], P('batch')
- grad_q_bias: float32 [768], P('batch')
- grad_k_weight: float32 [768, 768], P('batch')
- grad_v_weight: float32 [768, 768], P('batch')
- grad_v_bias: float32 [768], P('batch')
- grad_o_weight: float32 [768, 768], P('batch')
- grad_o_bias: float32 [768], P('batch')
- grad_norm1_gain: float32 [768], P('batch')
- grad_norm1_bias: float32 [768], P('batch')
- grad_up_weight: float32 [768, 3072], P('batch')
- grad_up_bias: float32 [3072], P('batch')
- grad_down_weight: float32 [3072, 768], P('batch')
- grad_down_bias: float32 [768], P('batch')
- grad_norm2_gain: float32 [768], P('batch')
- grad_norm2_bias: float32 [768], P('batch')
The draws below stay inside these ranges and needn't reach their ends.
Inputs may be any that keep to these rules, and one draw needn't show every extreme that they name: `seg_ids`: in each row the text numbers run from 0 to 3 without falling, every text present. `pos_ids`: each passage is the positive of exactly one query.
All inputs are finite; a program needn't handle non-finite values.
Results may differ from the reference program's by a relative error of at most 0.013.
Values may be sent and summed in bfloat16 or wider, within the bound.
No kernel may reach another device: no remote copies, remote signals or barrier semaphores. Data moves between devices by JAX's collectives and lax.ppermute only.
A program may use at most 192 MiB of HBM per device.

```python
import math
from functools import partial
import jax
import jax.numpy as jnp
import numpy as np
from jax import lax

D = 768
HEADS = 12
HD = 64
FF = 3072
LEN = 512
SEGS = 4
ROWS = 16
TEXTS = 64
N_STREAM = 2


def draw_tokens(key, part):
    key = jax.random.fold_in(key, 11)
    dir_key, amp_key, sign_key, noise_key = jax.random.split(key, 4)
    token_count = N_STREAM * ROWS * LEN
    directions = jax.random.normal(dir_key, (16, D), jnp.float32) * D ** (-0.5)
    amplitudes = 4.0 + 3.0 * jax.random.uniform(amp_key, (16,), jnp.float32)
    sign_flips = jax.random.rademacher(sign_key, (token_count, 16), jnp.float32)
    base_noise = 0.5 * jax.random.normal(noise_key, (token_count, D), jnp.float32)
    values = base_noise
    for column in range(16):
        values = values + sign_flips[:, column:column + 1] * amplitudes[column] * directions[column][None, :]
    values = jnp.clip(values, -6.0, 6.0)
    return values.reshape(N_STREAM, ROWS * LEN, D).astype(jnp.bfloat16)


def profile(number_of, total, reach, lean):
    portions = [(1 << 20) // math.isqrt(standing ** lean) + 1 for standing in range(2, number_of + 1)]
    spare, counts = total - reach - (number_of - 1), [1] * (number_of - 1)
    while spare > 0:
        free = [i for i in range(number_of - 1) if counts[i] < reach]
        whole, left = sum([portions[i] for i in free]), spare
        for i in free:
            extra = min(reach - counts[i], max(1, left * portions[i] // whole), spare)
            counts[i] = counts[i] + extra
            spare = spare - extra
    return np.array([reach] + counts)


def uneven_parts(key, amount, total, limit, lean):
    if amount == 2:
        one = jax.random.randint(key, (), max(1, total - limit), min(limit, total - 1) + 1)
        return jnp.stack([one, total - one])
    tallies = jnp.asarray(profile(amount, total, limit, lean), jnp.int32)
    couples = (amount - 1) // 2
    source_of, taker = tallies[1:1 + 2 * couples:2], tallies[2:2 + 2 * couples:2]
    margin = jnp.minimum(source_of - 1, limit - taker)
    passed = jax.random.randint(jax.random.fold_in(key, 1), (couples,), 0, 1 << 20) % (margin + 1)
    tallies = tallies.at[1:1 + 2 * couples:2].set(source_of - passed).at[2:2 + 2 * couples:2].set(taker + passed)
    return tallies[jax.random.permutation(jax.random.fold_in(key, 2), amount)]


def centred(own_key, extent, width, most, held_as=jnp.bfloat16):
    return jnp.clip(width * jax.random.normal(own_key, extent, jnp.float32), -most, most).astype(held_as)


def setup_inputs(seed: int = 0) -> dict:
    keys = jax.random.split(jax.random.key(seed), 19)
    tokens = draw_tokens(jax.random.fold_in(keys[18], 71), 0)
    seg_ids = jax.vmap(lambda own: jnp.searchsorted(jnp.cumsum(uneven_parts(own, SEGS, LEN, LEN // 2 + LEN // 4, 2)), jnp.arange(LEN), side="right"))(jax.random.split(keys[1], N_STREAM * ROWS)).reshape((N_STREAM, ROWS, LEN)).astype(jnp.int32)
    pos_ids = jax.random.permutation(keys[2], TEXTS).astype(jnp.int32)
    q_weight = centred(keys[3], (D, D), D ** -0.5, 0.21875)
    q_bias = centred(keys[4], (D,), 0.3, 1.796875)
    k_weight = centred(keys[5], (D, D), D ** -0.5, 0.21875)
    v_weight = centred(keys[6], (D, D), D ** -0.5, 0.21875)
    v_bias = centred(keys[7], (D,), 0.3, 1.796875)
    o_weight = centred(keys[8], (D, D), (D // 16) ** -0.5, 0.875)
    o_bias = centred(keys[9], (D,), 0.3, 1.796875)
    norm1_gain = jnp.clip(1.0 + 0.1 * jax.random.normal(keys[10], (D,), jnp.float32), 0.5, 1.5).astype(jnp.bfloat16)
    norm1_bias = centred(keys[11], (D,), 0.3, 1.796875)
    up_weight = centred(keys[12], (D, FF), D ** -0.5, 0.21875)
    up_bias = centred(keys[13], (FF,), 0.3, 1.796875)
    down_weight = centred(keys[14], (FF, D), FF ** -0.5, 0.109375)
    down_bias = centred(keys[15], (D,), 0.3, 1.796875)
    norm2_gain = jnp.clip(1.0 + 0.1 * jax.random.normal(keys[16], (D,), jnp.float32), 0.5, 1.5).astype(jnp.bfloat16)
    norm2_bias = centred(keys[17], (D,), 0.2, 1.1953125)
    return dict(tokens=tokens, seg_ids=seg_ids, pos_ids=pos_ids, q_weight=q_weight, q_bias=q_bias, k_weight=k_weight, v_weight=v_weight, v_bias=v_bias, o_weight=o_weight, o_bias=o_bias, norm1_gain=norm1_gain, norm1_bias=norm1_bias, up_weight=up_weight, up_bias=up_bias, down_weight=down_weight, down_bias=down_bias, norm2_gain=norm2_gain, norm2_bias=norm2_bias)


@jax.custom_vjp
def low(v):
    return lax.optimization_barrier(v.astype(jnp.bfloat16)).astype(jnp.float32)

@jax.custom_vjp
def low_back(v):
    return v

def low_keep(v):
    return (low(v), None)

def low_pass(kept, grad):
    return (grad,)

def back_keep(v):
    return (v, None)

def back_low(kept, grad):
    return (low(grad),)
low.defvjp(low_keep, low_pass)
low_back.defvjp(back_keep, back_low)

def layer_norm(values_in, scale_gain, shift_bias):
    center = lax.optimization_barrier(jnp.mean(values_in, axis=-1, keepdims=True))
    offset = values_in - center
    spread = lax.optimization_barrier(jnp.mean(offset * offset, axis=-1, keepdims=True))
    return offset * lax.rsqrt(spread + 1e-06) * scale_gain + shift_bias

def product(left, right):
    return jnp.dot(left, right, precision=lax.Precision.HIGHEST)

def encode_row(weights, row_tokens, row_segs):
    q_weight, q_bias, k_weight, v_weight, v_bias, o_weight, o_bias, norm1_gain, norm1_bias, up_weight, up_bias, down_weight, down_bias, norm2_gain, norm2_bias = weights
    queries = low_back(low(product(row_tokens, q_weight) + q_bias)).reshape(LEN, HEADS, HD)
    keys_row = low_back(low(product(row_tokens, k_weight))).reshape(LEN, HEADS, HD)
    values_row = low_back(low(product(row_tokens, v_weight) + v_bias)).reshape(LEN, HEADS, HD)
    scores = jnp.einsum('qhd,khd->hqk', queries, keys_row, precision=lax.Precision.HIGHEST) * 0.125
    scores = low_back(scores)
    same_text = row_segs[:, None] == row_segs[None, :]
    scores = jnp.where(same_text[None], scores, -1000000000.0)
    shifted = scores - lax.optimization_barrier(jnp.max(scores, axis=-1, keepdims=True))
    exponent = jnp.exp(shifted)
    attention = low(exponent / lax.optimization_barrier(jnp.sum(exponent, axis=-1, keepdims=True)))
    mixture = jnp.einsum('hqk,khd->qhd', attention, values_row, precision=lax.Precision.HIGHEST).reshape(LEN, D)
    mixture = low_back(low(mixture))
    attended = low_back(product(mixture, o_weight) + o_bias)
    first_out = layer_norm(row_tokens + attended, norm1_gain, norm1_bias)
    hidden = low_back(product(low(first_out), up_weight) + up_bias)
    active = low(jax.nn.gelu(hidden, approximate=False))
    branch = low_back(product(active, down_weight) + down_bias)
    second_out = layer_norm(first_out + branch, norm2_gain, norm2_bias)
    member = (row_segs[:, None] == jnp.arange(SEGS)[None, :]).astype(jnp.float32)
    pooled = product(member.T, second_out) / lax.optimization_barrier(jnp.sum(member, axis=0))[:, None]
    embedded = pooled * lax.rsqrt(lax.optimization_barrier(jnp.sum(pooled * pooled, axis=-1, keepdims=True)) + 1e-06)
    return (low(embedded), second_out)

def forward(tokens_float, seg_ids, pos_ids, weights):
    rows_all = tokens_float.reshape(-1, LEN, D)
    segs_all = seg_ids.reshape(-1, LEN)
    encoder = jax.checkpoint(partial(encode_row, weights))

    def advance(carry, item):
        embedded, second_out = encoder(item[0], item[1])
        return (carry, (embedded, second_out))
    carry_init = jnp.zeros((), jnp.float32)
    unused, (embeds, seconds) = lax.scan(advance, carry_init, (rows_all, segs_all))
    texts_all = embeds.reshape(2, -1, D)
    scores = low_back(product(texts_all[0], texts_all[1].T) * 100.0)
    row_peak = lax.optimization_barrier(jnp.max(scores, axis=-1, keepdims=True))
    log_total = row_peak[:, 0] + jnp.log(lax.optimization_barrier(jnp.sum(jnp.exp(scores - row_peak), axis=-1)))
    target = jnp.take_along_axis(scores, pos_ids[:, None], axis=1)[:, 0]
    return (jnp.mean(log_total - target), seconds.reshape(tokens_float.shape))

def reference(tokens, seg_ids, pos_ids, q_weight, q_bias, k_weight, v_weight, v_bias, o_weight, o_bias, norm1_gain, norm1_bias, up_weight, up_bias, down_weight, down_bias, norm2_gain, norm2_bias):
    weights = tuple((item.astype(jnp.float32) for item in (q_weight, q_bias, k_weight, v_weight, v_bias, o_weight, o_bias, norm1_gain, norm1_bias, up_weight, up_bias, down_weight, down_bias, norm2_gain, norm2_bias)))

    def objective(tokens_float, *weight_list):
        return forward(tokens_float, seg_ids, pos_ids, weight_list)
    loss, pullback, second_all = jax.vjp(objective, tokens.astype(jnp.float32), *weights, has_aux=True)
    grads = pullback(jnp.ones((), jnp.float32))
    return (loss, second_all.astype(jnp.bfloat16), grads[0], grads[1], grads[2], grads[3], grads[4], grads[5], grads[6], grads[7], grads[8], grads[9], grads[10], grads[11], grads[12], grads[13], grads[14], grads[15])
```

```python
import functools

import jax
import jax.numpy as jnp
import numpy as np
from jax import lax
from jax.experimental import pallas as pl
from jax.experimental.pallas import tpu as pltpu
from jax.sharding import PartitionSpec as P

D = 768
HEADS = 12
HD = 64
LEN = 512
SEGS = 4
FF = 3072
HALF = D // 2
FH = FF // 2
PAIRS = HEADS // 2
ROWS8 = 8
MIB = 1 << 20
AXES = ("stream", "batch")
BF = jnp.bfloat16
F32 = jnp.float32
EPS = 1e-06
LOG2E = 1.4426950408889634
VECTORS = 16
COST_RATE = 1.15e9
COSTS = {"loss": 3.0, "hidden": 3.5, "down": 60.0, "first": 60.0, "up": 0.1, "heads0": 0.1, "heads1": 30.0, "qkv": 0.1, "input": 0.1, "add": 3.0, "end": 0.6}
PLANS = {
    "a": ("xwyz", "xzyw"),
    "b": ("xzyw", "zyxw"),
    "u": ("yxwz", "zxyw"),
    "q": ("zyxw", "zxyw"),
    "r": ("xyzw", "yxwz"),
}
ORDER = ("down", "first", "up", "heads0", "heads1", *"abu", "qkv", "input", *"abuqrabuqrabuqr", "end_down", "q", "end_up", "r", "end_qkv")


def shape_of(shape, dtype):
    return jax.ShapeDtypeStruct(tuple(shape), dtype)


def cost(micros):
    return pl.CostEstimate(flops=int(micros * COST_RATE) + 1, bytes_accessed=0, transcendentals=0)


class Pieces:
    def __init__(self, ref, places):
        self.refs, self.places = [ref] * len(places), places

    def get(self, i=0):
        return window(self.refs[i], self.places[i])


def near(x):
    return ("near", x)


def after(*arrays):
    return [("after", x) for x in arrays]


def late(x, *places):
    return ("late", x, places or ((),))


def window(ref, index):
    return ref.at[index] if index != () else ref


def call(body, outs, args, name, micros, limit=8, scratch=()):
    spaces = {"near": pltpu.VMEM, "after": pl.ANY, "late": pltpu.VMEM}

    def whole(*refs):
        ins, rest = refs[: len(args)], refs[len(args) :]
        operands = []
        for arg, ref in zip(args, ins):
            if arg[0] == "late":
                operands.append(Pieces(ref, [x() if callable(x) else x for x in arg[2]]))
            elif arg[0] != "after":
                operands.append(ref)
        body(*operands, *rest)

    return pl.pallas_call(
        whole,
        out_shape=outs,
        in_specs=[pl.BlockSpec(memory_space=spaces[arg[0]]) for arg in args],
        out_specs=[pl.BlockSpec(memory_space=pltpu.VMEM)] * len(outs),
        scratch_shapes=list(scratch),
        compiler_params=pltpu.CompilerParams(vmem_limit_bytes=limit * MIB),
        cost_estimate=cost(micros),
        name=name,
    )(*[arg[1] for arg in args])


def lanes_of(start, width):
    return (slice(None), slice(start, start + width))


def dot(left, right):
    return jnp.dot(left, right, preferred_element_type=F32)


def dot_nt(left, right):
    return lax.dot_general(left, right, (((1,), (1,)), ((), ())), preferred_element_type=F32)


def dot_tn(left, right):
    return lax.dot_general(left, right, (((0,), (0,)), ((), ())), preferred_element_type=F32)


def wide(ref):
    return ref[...].astype(F32)


FIRST, MIXED, TOKENS, STACK = 0, D, 2 * D, 3 * D


def normalize(x):
    center = jnp.mean(x, axis=-1, keepdims=True)
    offset = x - center
    spread = jnp.mean(offset * offset, axis=-1, keepdims=True)
    scale = lax.rsqrt(spread + EPS)
    return offset * scale, scale


def lane(ref):
    return ref[...].astype(F32).reshape(1, -1)


def segment_counts(seg_row, seg):
    return jnp.sum((seg_row == seg).astype(F32), axis=-1, keepdims=True)


def column_of(seg_row):
    return jnp.broadcast_to(seg_row.astype(F32), (128, LEN)).T[:, :1].astype(jnp.int32)


def forward_body(
    tok_h, seg, qw_h, kw_h, vw_h, ow_h, uw_h, dw_h, qb, vb, ob, gain1, shift1, ub, db, gain2, shift2,
    embeds, pooled_out, scale1, scale2, out_h, act_h, stack_h, q_h, k_h, v_h, p_h, slope_h, normed1_h, normed2_h,
    qw, kw, vw, ow, uw, dw, out, act, stack, q, k, v, p, slope, normed1, normed2, bias, kept, sems,
):
    tokens = stack.at[:, TOKENS:STACK]
    loads = [
        pltpu.make_async_copy(src, dst, sems.at[i])
        for i, (src, dst) in enumerate(
            ((tok_h, tokens), (qw_h, qw), (kw_h, kw), (vw_h, vw), (ow_h, ow), (uw_h, uw), (dw_h, dw))
        )
    ]
    for load in loads:
        load.start()
    stores = []

    def store(source, home):
        copy = pltpu.make_async_copy(source, home, sems.at[len(loads) + len(stores)])
        copy.start()
        stores.append(copy)

    owner = column_of(seg[...])
    bias[...] = jnp.where(owner == seg[...], 0.0, -1e30)
    loads[0].wait()
    x = stack[:, TOKENS:STACK]
    for weight, load, shift, ref, home in (
        (qw, loads[1], qb, q, q_h), (kw, loads[2], None, k, k_h), (vw, loads[3], vb, v, v_h)
    ):
        load.wait()
        y = dot(x, weight[...])
        ref[...] = (y if shift is None else y + lane(shift)).astype(BF)
        store(ref, home)

    first_rows = lax.broadcasted_iota(jnp.int32, (LEN, 2 * HD), 1) < HD

    def pair(i, carry):
        lanes = pl.ds(pl.multiple_of(i * 2 * HD, 2 * HD), 2 * HD)
        q2, k2 = q[:, lanes], k[:, lanes]
        turned = v[:, lanes].T
        zero = jnp.zeros_like(q2)
        parts = []
        for half in range(2):
            keep = first_rows if half == 0 else jnp.logical_not(first_rows)
            scores = dot_nt(jnp.where(keep, k2, zero), q2) + bias[...]
            peak = jnp.max(scores, axis=0, keepdims=True)
            expo = jnp.exp2((scores - peak) * (0.125 * LOG2E))
            total = jnp.sum(expo, axis=0, keepdims=True)
            probs = (expo * (1.0 / total)).astype(BF)
            p[2 * i + half] = probs
            parts.append(dot(turned[half * HD : (half + 1) * HD], probs))
        mixed = jnp.concatenate(parts, axis=0).T.astype(BF)
        stack[:, pl.ds(pl.multiple_of(MIXED + i * 2 * HD, 2 * HD), 2 * HD)] = mixed
        return carry

    lax.fori_loop(0, PAIRS, pair, 0)
    store(p, p_h)
    loads[4].wait()
    x = stack[:, TOKENS:STACK].astype(F32) + dot(stack[:, MIXED:TOKENS], ow[...]) + lane(ob)
    n, s = normalize(x)
    normed1[...] = n.astype(BF)
    store(normed1, normed1_h)
    scale1[...] = s
    kept[...] = n * lane(gain1) + lane(shift1)
    stack[:, FIRST:MIXED] = kept[...].astype(BF)
    store(stack, stack_h)
    loads[5].wait()
    loads[6].wait()
    low = stack[:, FIRST:MIXED]
    total = None
    for start in range(0, FF, D):
        cols = slice(start, start + D)
        hidden = dot(low, uw[:, cols]) + ub[cols].astype(F32).reshape(1, -1)
        phi = 0.5 * (1.0 + lax.erf(hidden * 0.7071067811865476))
        low_act = (hidden * phi).astype(BF)
        act[:, cols] = low_act
        density = jnp.exp2(hidden * hidden * (-0.5 * LOG2E)) * 0.3989422804014327
        slope[:, cols] = (phi + hidden * density).astype(BF)
        part = dot(low_act, dw[cols, :])
        total = part if total is None else total + part
    store(act, act_h)
    store(slope, slope_h)
    n, s = normalize(kept[...] + total + lane(db))
    normed2[...] = n.astype(BF)
    store(normed2, normed2_h)
    scale2[...] = s
    second = n * lane(gain2) + lane(shift2)
    out[...] = second.astype(BF)
    store(out, out_h)
    rows = lax.broadcasted_iota(jnp.int32, (ROWS8, D), 0)
    pooled = jnp.zeros((ROWS8, D), F32)
    for text in range(SEGS):
        mean = jnp.sum(jnp.where(owner == text, second, 0.0), axis=0, keepdims=True) / segment_counts(seg[...], text)
        pooled = jnp.where(rows == text, mean, pooled)
    pooled_out[...] = pooled
    embed = (pooled * lax.rsqrt(jnp.sum(pooled * pooled, axis=-1, keepdims=True) + EPS)).astype(BF)[:SEGS]
    for i in range(embeds.shape[0]):
        embeds[i] = embed
    for copy in stores:
        copy.wait()


def forward(devices, tok, seg, weights, vectors):
    here, away = pl.BlockSpec(memory_space=pltpu.VMEM), pl.BlockSpec(memory_space=pltpu.HBM)
    low, full, square = ((LEN, D), BF), ((LEN, D), F32), ((D, D), BF)
    outs = [((devices, SEGS, D), BF), ((ROWS8, D), F32), ((LEN, 1), F32), ((LEN, 1), F32)]
    saved = [low, ((LEN, FF), BF), ((LEN, STACK), BF), low, low, low, ((HEADS, LEN, LEN), BF), ((LEN, FF), BF), low, low]
    scratch = [square] * 4 + [((D, FF), BF), ((FF, D), BF)] + saved + [((LEN, LEN), F32), full]
    return pl.pallas_call(
        forward_body,
        out_shape=[shape_of(*x) for x in outs + saved],
        in_specs=[away, here] + [away] * 6 + [here] * 9,
        out_specs=[here] * len(outs) + [away] * len(saved),
        scratch_shapes=[pltpu.VMEM(*x) for x in scratch] + [pltpu.SemaphoreType.DMA((7 + len(saved),))],
        compiler_params=pltpu.CompilerParams(vmem_limit_bytes=56 * MIB),
        cost_estimate=cost(25.0),
        name="forward",
    )(tok, seg, *weights, *vectors)


def half_of(ref, index, width):
    return ref[:, pl.ds(pl.multiple_of(index * width, 128), width)]


def norm_back(grad_out, gain, normed, scale):
    weighted = grad_out * gain
    mean_plain = jnp.mean(weighted, axis=-1, keepdims=True)
    mean_cross = jnp.mean(weighted * normed, axis=-1, keepdims=True)
    return scale * (weighted - mean_plain - normed * mean_cross)


def column_sum(x):
    return jnp.sum(x.astype(F32), axis=0, keepdims=True)


def loss_body(texts, normed, scale, pooled_in, gathered, pos, seg, gain, loss, branch, branch_send, sums, tall):
    stream, batch = lax.axis_index("stream"), lax.axis_index("batch")
    for i in range(gathered.shape[0]):
        tall[i, :SEGS] = gathered[i].astype(F32)
        tall[i, SEGS:] = jnp.zeros((ROWS8 - SEGS, D), F32)
    every = tall[...].reshape(4 * texts, D).astype(BF)
    span = 2 * texts
    row = lax.broadcasted_iota(jnp.int32, (texts, span), 0)
    col = lax.broadcasted_iota(jnp.int32, (texts, span), 1)
    pick = (col == (row // SEGS) * ROWS8 + row % SEGS).astype(F32).astype(BF)
    query = dot(pick, every[:span]).astype(BF)
    passage = dot(pick, every[span:]).astype(BF)
    scores = dot_nt(passage, query) * 100.0
    peak = jnp.max(scores, axis=0, keepdims=True)
    log_total = peak + jnp.log(jnp.sum(jnp.exp(scores - peak), axis=0, keepdims=True))
    chosen = (lax.broadcasted_iota(jnp.int32, (texts, texts), 0) == pos[...]).astype(F32)
    losses = log_total - jnp.sum(chosen * scores, axis=0, keepdims=True)
    loss[...] = jnp.sum(losses, axis=1, keepdims=True) / texts
    grad_scores = ((jnp.exp(scores - log_total) - chosen) / texts).astype(BF)
    row = lax.broadcasted_iota(jnp.int32, (ROWS8, texts), 0)
    col = lax.broadcasted_iota(jnp.int32, (ROWS8, texts), 1)
    mine = jnp.logical_and(col == batch * SEGS + row, row < SEGS).astype(F32).astype(BF)
    to_query = dot(dot_nt(mine, grad_scores).astype(BF), passage)
    to_passage = dot(dot(mine, grad_scores).astype(BF), query)
    grad_embed = jnp.where(stream == 0, to_query, to_passage) * 100.0
    pooled = pooled_in.get()[...]
    inverse = lax.rsqrt(jnp.sum(pooled * pooled, axis=-1, keepdims=True) + EPS)
    cross = jnp.sum(grad_embed * pooled, axis=-1, keepdims=True)
    grad_pooled = inverse * grad_embed - pooled * (inverse * inverse * inverse * cross)
    owner = column_of(seg[...])
    grad_second = jnp.zeros((LEN, D), F32)
    for text in range(SEGS):
        share = grad_pooled[text : text + 1] / segment_counts(seg[...], text)
        grad_second = jnp.where(owner == text, share, grad_second)
    n = normed.get()[...].astype(F32)
    resid = norm_back(grad_second, lane(gain), n, scale.get()[...])
    branch[...] = resid.astype(BF)
    branch_send[...] = half_of(branch, 1 - stream, HALF)
    sums[0:1] = column_sum(grad_second * n)
    sums[1:2] = column_sum(grad_second)
    sums[2:3] = column_sum(branch[...])


def hidden_body(dw, slope, branch, grad_hidden, send, sums):
    for j in range(len(dw.refs)):
        cols = slice(j * D, (j + 1) * D)
        grad = (dot_nt(branch[...], dw.get(j)[...]) * slope.get(j)[...].astype(F32)).astype(BF)
        grad_hidden[:, cols] = grad
        sums[:, cols] = column_sum(grad)
    send[...] = half_of(grad_hidden, 1 - lax.axis_index("stream"), FH)


def where_to(plan, i):
    stream, relative = lax.axis_index("stream"), lax.axis_index("batch") ^ i
    slots = []
    for bits in plan:
        last = len(bits) - 1
        slots.append(sum((((relative >> bit) & 1) << (last - step)) for step, bit in enumerate(bits)))
    return jnp.where(stream == 0, slots[0], slots[1])


def put_chunk(part, slot, keep, send, lanes):
    here = keep.shape[0]

    @pl.when(slot < here)
    def _():
        keep[slot, :, lanes] = part

    @pl.when(slot >= here)
    def _():
        send[slot - here, :, lanes] = part


def place_rows(total, first, rows, groups, outs, start):
    if groups is None:
        outs[0][first : first + total.shape[0], start : start + total.shape[1]] = total
        return
    low = total.astype(BF)
    for n, (plan, top, height, left, width) in enumerate(groups):
        begin, end = max(left, start), min(left + width, start + total.shape[1])
        if begin >= end:
            continue
        for i in range(total.shape[0] // rows):
            piece = low[i * rows + top : i * rows + top + height, begin - start : end - start]
            put_chunk(piece, where_to(plan, first // rows + i), outs[2 * n], outs[2 * n + 1], slice(begin - left, end - left))


def outer_body(rows, groups, counts, left, left_other, *refs):
    rights, outs = refs[: 2 * len(counts)], refs[2 * len(counts) :]
    start = piece = 0
    for i, count in enumerate(counts):
        right, right_other = rights[2 * i : 2 * i + 2]
        columns = right_other.shape[1]
        mine = right[...] if right.shape[1] == columns else half_of(right, lax.axis_index("stream"), columns)
        other = right_other[...]
        for j in range(count):
            total = dot_tn(left.get(piece)[...], mine) + dot_tn(left_other.get(piece)[...], other)
            piece += 1
            place_rows(total, j * D, rows, groups, outs, start)
        start += columns


def first_body(uw, normed, scale, grad_hidden, branch, gain, attn, sums):
    grad_first = branch[...].astype(F32)
    for j in range(len(uw.refs)):
        grad_first += dot_nt(grad_hidden[:, j * D : (j + 1) * D], uw.get(j)[...])
    n = normed.get()[...].astype(F32)
    resid = norm_back(grad_first, lane(gain), n, scale.get()[...])
    attn[...] = resid.astype(BF)
    sums[0:1] = column_sum(grad_first * n)
    sums[1:2] = column_sum(grad_first)
    sums[2:3] = column_sum(attn[...])


def half_index(which):
    stream = lax.axis_index("stream")
    return stream if which else 1 - stream


def head_lanes(which):
    return lambda: (slice(None), pl.ds(pl.multiple_of(half_index(which) * HALF, 128), HALF))


def head_rows(which):
    return lambda: pl.ds(pl.multiple_of(half_index(which) * HALF, 128), HALF)


def head_pair(which, i):
    return lambda: pl.ds(half_index(which) * (HEADS // 2) + 2 * i, 2)


def attend_back_body(which, ow, v, k, q, p, attn, grads_qk, grads_v, sums):
    grad_mixed = dot_nt(attn[...], ow.get()[...]).astype(BF)
    first_lanes = lax.broadcasted_iota(jnp.int32, (LEN, 2 * HD), 1) < HD
    for i in range(PAIRS // 2):
        lanes = slice(i * 2 * HD, (i + 1) * 2 * HD)
        g2, v2, k2, q2 = grad_mixed[:, lanes], v.get()[:, lanes], k.get()[:, lanes], q.get()[:, lanes]
        zero = jnp.zeros_like(q2)
        turned = k2.T
        tq, tk, tv = [], None, None
        for half in range(2):
            keep = first_lanes if half == 0 else jnp.logical_not(first_lanes)
            probs = p.get(i)[half]
            g = jnp.where(keep, g2, zero)
            weighted = dot_nt(v2, g) * probs.astype(F32)
            inner = jnp.sum(weighted, axis=0, keepdims=True)
            raw = (weighted - probs.astype(F32) * inner).astype(BF)
            tq.append(dot(turned[half * HD : (half + 1) * HD], raw))
            parts = (dot(raw, jnp.where(keep, q2, zero)), dot(probs, g))
            tk, tv = parts if half == 0 else (tk + parts[0], tv + parts[1])
        for j, grad in enumerate((jnp.concatenate(tq, axis=0).T * 0.125, tk * 0.125, tv)):
            ref, start = (grads_v, i * 2 * HD) if j == 2 else (grads_qk, j * HALF + i * 2 * HD)
            ref[:, start : start + 2 * HD] = grad.astype(BF)
    grads_v[:, HALF:] = half_of(attn, half_index(which), HALF)
    sums[0:1] = column_sum(grads_qk[:, :HALF])
    sums[1:2] = column_sum(grads_v[:, :HALF])


VEC = ("gain2", "bias2", "down", "gain1", "bias1", "out", "query", "value")


def whole_rows(stream, away, own):
    return jnp.where(stream == 0, jnp.concatenate([own, away], axis=1), jnp.concatenate([away, own], axis=1))


def qkv_outer_body(rows, groups, left, left_other, *refs):
    rights, (sums2, sums1, sums_away, sums_own, sums_up), outs = refs[:4], refs[4:9], refs[9:]
    if groups is not None:
        plan, _, _, first_lane, _ = groups[-1]
        blank = jnp.zeros((128 - len(VEC), D), F32)
        sums0 = whole_rows(lax.axis_index("stream"), sums_away[0:2], sums_own[0:2])
        turned = jnp.concatenate([sums2[0:3], sums1[0:3], sums0, blank], axis=0).T
        tall = jnp.broadcast_to(sums_up[...], (128, FF)).T.reshape(D // rows, FF // D, rows, 128)
        slot = lax.broadcasted_iota(jnp.int32, (rows, 128), 1)
        for i in range(D // rows):
            piece = turned[i * rows : (i + 1) * rows]
            for part in range(FF // D):
                piece = jnp.where(slot == len(VEC) + part, tall[i, part], piece)
            lanes = slice(4 * HALF - first_lane, 4 * HALF - first_lane + 128)
            put_chunk(piece.astype(BF), where_to(plan, i), outs[-2], outs[-1], lanes)
    own_qk, own_v, other_qk, other_v = rights
    start = 0
    for i, (own, other) in enumerate(((own_qk, other_qk), (own_v, other_v))):
        for j in range(2):
            lanes, piece = slice(j * HALF, (j + 1) * HALF), i * j
            total = dot_tn(left.get(piece)[...], own[:, lanes]) + dot_tn(left_other.get(piece)[...], other[:, lanes])
            place_rows(total, 0, rows, groups, outs, start)
            start += HALF


def input_body(qw, kw, vw, attn, *refs):
    out = refs[-1]
    total = attn[...].astype(F32)
    for i, weight in enumerate((qw, kw, vw)):
        for which in range(2):
            grads = refs[2 * which + i // 2][:, i % 2 * HALF : (i % 2 + 1) * HALF]
            total += dot_nt(grads, weight.get(which)[...])
    out[...] = total


def add_body(keep, arrived, *outs):
    if len(outs) == 1:
        outs[0][...] = (wide(keep) + wide(arrived)).astype(BF)
        return
    half = outs[0].shape[0]
    outs[0][...] = (keep[:half].astype(F32) + arrived[:half].astype(F32)).astype(BF)
    outs[1][...] = (keep[half:].astype(F32) + arrived[half:].astype(F32)).astype(BF)


def final_body(count, pieces, vectors, *refs):
    mine, other, outs = refs[:count], refs[count : 2 * count], refs[2 * count :]
    swap = lax.axis_index("stream") != 0
    for ref, parts in zip(outs, pieces):
        middle = ref.shape[1] // 2
        at = {}
        for which, lane_from, lanes, top in parts:
            a, b = mine[which][:, lane_from : lane_from + lanes], other[which][:, lane_from : lane_from + lanes]
            rows, begin = slice(top, top + a.shape[0]), at.get(top, 0)
            ref[rows, begin : begin + lanes] = jnp.where(swap, b, a).astype(F32)
            ref[rows, middle + begin : middle + begin + lanes] = jnp.where(swap, a, b).astype(F32)
            at[top] = begin + lanes
    if vectors is not None:
        both = (mine[-1][:, vectors:].astype(F32) + other[-1][:, vectors:].astype(F32)).T
        for i, ref in enumerate(outs[len(pieces) :]):
            if i < len(VEC):
                ref[...] = both[i]
            else:
                ref[...] = jnp.concatenate([both[i + j : i + j + 1] for j in range(FF // D)], axis=1).reshape(-1)


def swap_cores(x):
    return lax.ppermute(x, "stream", [(0, 1), (1, 0)])


AXIS_BITS = {"x": 0, "y": 1, "z": 2, "w": 3}


def bit_plan(plan, batches):
    count = batches.bit_length() - 1
    return [[AXIS_BITS[axis] for axis in order] if count == len(order) else list(range(count)) for order in plan]


def halve_send(send, plan, batches, step):
    pairs = [
        (core * batches + b, core * batches + (b ^ (1 << plan[core][step]))) for core in range(2) for b in range(batches)
    ]
    return lax.ppermute(send, AXES, pairs)


def local(
    batches,
    tokens,
    seg_ids,
    pos_ids,
    q_weight,
    q_bias,
    k_weight,
    v_weight,
    v_bias,
    o_weight,
    o_bias,
    norm1_gain,
    norm1_bias,
    up_weight,
    up_bias,
    down_weight,
    down_bias,
    norm2_gain,
    norm2_bias,
):
    texts = pos_ids.shape[0]
    rows = D // batches
    chunked = rows % 16 == 0 and batches & (batches - 1) == 0
    stages = batches.bit_length() - 1
    tok, seg, pos = tokens.reshape(LEN, D), seg_ids.reshape(1, LEN), pos_ids.reshape(1, texts)
    low, sums = shape_of((LEN, D), BF), shape_of((ROWS8, D), F32)
    low_half = shape_of((LEN, HALF), BF)
    wide_low = shape_of((LEN, FF), BF)
    tall = FF // batches
    cuts = {
        "a": ("down", 0, tall // 2, 0, HALF),
        "b": ("down", tall // 2, tall // 2, 0, HALF),
        "u": ("up", 0, rows, 0, FH),
        "q": ("qkv", 0, rows, 0, 2 * HALF),
        "r": ("qkv", 0, rows, 2 * HALF, 2 * HALF + 128),
    }
    plans = {name: bit_plan(plan, batches) for name, plan in PLANS.items()}
    token = []

    def run(body, outs, args, name, micros, limit=8, **more):
        results = call(body, outs, args + after(*token), name, micros, limit if chunked else 48, **more)
        token[:] = [results[0]]
        return results

    embeds, pooled, scale1, scale2, hidden_out, act, stack, q, k, v, p, slope, normed1, normed2 = forward(
        2 * batches,
        tok,
        seg,
        (q_weight, k_weight, v_weight, o_weight, up_weight, down_weight),
        (q_bias, v_bias, o_bias, norm1_gain, norm1_bias, up_bias, down_bias, norm2_gain, norm2_bias),
    )
    gathered = lax.all_to_all(embeds, AXES, split_axis=0, concat_axis=0)
    act_other = swap_cores(act)
    stack_other = swap_cores(stack)
    loss, branch, branch_send, sums2 = run(
        functools.partial(loss_body, texts),
        [shape_of((1, 1), F32), low, low_half, sums],
        [late(normed2), late(scale2), late(pooled), near(gathered), near(pos), near(seg), near(norm2_gain)],
        "loss",
        COSTS["loss"],
        scratch=[pltpu.VMEM((2 * batches, ROWS8, D), F32)],
    )
    branch_other = swap_cores(branch_send)
    grad_hidden, hidden_send, sums_up = run(
        hidden_body,
        [wide_low, shape_of((LEN, FH), BF), shape_of((1, FF), F32)],
        [
            late(down_weight, *[(slice(j, j + D), slice(None)) for j in range(0, FF, D)]),
            late(slope, *[lanes_of(j, D) for j in range(0, FF, D)]),
            near(branch),
        ],
        "hidden",
        COSTS["hidden"],
    )
    hidden_other = swap_cores(hidden_send)
    held, arriving, step_of, kept = {}, {}, {}, {}

    def send(name):
        if step_of[name] < stages:
            arriving[name] = halve_send(held[name][-1], plans[name], batches, step_of[name])
        else:
            arriving[name] = swap_cores(held[name][0][0])

    def add(name):
        keep, arrived = held[name][0], arriving[name]
        count = keep.shape[0]
        sizes = [count // 2] * 2 if count > 1 else [1]
        outs = [shape_of((size,) + keep.shape[1:], BF) for size in sizes]
        step_of[name] += 1
        held[name] = run(add_body, outs, [near(keep), near(arrived)], f"{name}_add{step_of[name]}", COSTS["add"])
        send(name)

    def outer(product, body, size, columns, own, other, starts, rights, others=()):
        windows = [lanes_of(start, D) for start in starts]
        args = [late(own, *windows), late(other, *windows)] + [near(x) for x in rights] + [near(x) for x in others]
        height = size // batches
        if not chunked:
            outs = [shape_of((size, columns), F32)]
            kept[product] = run(functools.partial(body, height, None), outs, args, f"outer_{product}", COSTS[product], 12)[0]
            return
        names = [name for name, cut in cuts.items() if cut[0] == product]
        groups = [(plans[name],) + cuts[name][1:] for name in names]
        outs = [shape_of((batches // 2, cuts[name][2], cuts[name][4]), BF) for name in names for _ in range(2)]
        results = run(functools.partial(body, height, groups), outs, args, f"outer_{product}", COSTS[product], 12)
        for i, name in enumerate(names):
            held[name], step_of[name] = results[2 * i : 2 * i + 2], 0
            send(name)

    def plain(*counts):
        return lambda height, groups, *refs: outer_body(height, groups, counts, *refs)

    def down():
        outer("down", plain(FF // D), FF, HALF, act, act_other, range(0, FF, D), [branch, branch_other])

    def first():
        kept["attn"], kept["sums1"] = run(
            first_body,
            [low, sums],
            [
                late(up_weight, *[lanes_of(j, D) for j in range(0, FF, D)]),
                late(normed1),
                late(scale1),
                near(grad_hidden),
                near(branch),
                near(norm1_gain),
            ],
            "first",
            COSTS["first"],
        )

    def up():
        outer("up", plain(1), D, FH, stack, stack_other, (FIRST,), [grad_hidden, hidden_other])

    def heads(which):
        lanes = head_lanes(which)
        *kept["grads", which], kept["sums", which] = run(
            functools.partial(attend_back_body, which),
            [low, low, shape_of((ROWS8, HALF), F32)],
            [
                late(o_weight, head_rows(which)),
                late(v, lanes),
                late(k, lanes),
                late(q, lanes),
                late(p, *[head_pair(which, i) for i in range(PAIRS // 2)]),
                near(kept["attn"]),
            ],
            f"attend_back{which}",
            COSTS[f"heads{which}"],
            10,
        )
        if which == 0:
            kept["grads_other"] = [swap_cores(x) for x in kept["grads", 0]]

    def qkv():
        vectors = [sums2, kept["sums1"], kept["sums", 0], kept["sums", 1], sums_up]
        columns = 4 * HALF + (128 if chunked else 0)
        rights = kept["grads", 1] + kept["grads_other"]
        outer("qkv", qkv_outer_body, D, columns, stack, stack_other, (TOKENS, MIXED), rights, vectors)

    def grad_tokens():
        weights = [late(w, head_lanes(0), head_lanes(1)) for w in (q_weight, k_weight, v_weight)]
        grads = [near(x) for x in [kept["attn"]] + kept["grads", 0] + kept["grads", 1]]
        kept["input"] = run(input_body, [shape_of((LEN, D), F32)], weights + grads, "input", COSTS["input"])[0]

    def finish(product, names, pieces, vectors=None):
        if chunked:
            mine, other = [held[name][0][0] for name in names], [arriving[name] for name in names]
        else:
            share = lax.psum_scatter(kept[product], "batch", scatter_dimension=0, tiled=True).astype(BF)
            mine, other = [share], [swap_cores(share)]
        height = (FF if product == "down" else D) // batches
        outs = [shape_of((height, 2 * sum(x[2] for x in parts if x[3] == 0)), F32) for parts in pieces]
        if vectors is not None:
            outs += [shape_of((rows,), F32)] * len(VEC) + [shape_of((tall,), F32)]
        args = [near(x) for x in mine + other]
        return run(functools.partial(final_body, len(mine), pieces, vectors), outs, args, f"final_{names[-1]}", COSTS["end"])

    def finish_down():
        pieces = [(0, 0, HALF, 0), (1, 0, HALF, tall // 2)] if chunked else [(0, 0, HALF, 0)]
        kept["g_down"] = finish("down", "ab", [pieces])[0]

    def finish_up():
        kept["g_up"] = finish("up", "u", [[(0, 0, FH, 0)]])[0]

    def finish_qkv():
        where = ((0, 0), (0, HALF), (1, 0), (1, HALF)) if chunked else [(0, i * HALF) for i in range(4)]
        pieces = [[(which, start, HALF, 0)] for which, start in where]
        results = finish("qkv", "qr", pieces, 2 * HALF if chunked else None)
        kept["g_q"], kept["g_k"], kept["g_v"], kept["g_o"], *kept["vec"] = results

    work = {
        "down": down,
        "first": first,
        "up": up,
        "heads0": lambda: heads(0),
        "heads1": lambda: heads(1),
        "qkv": qkv,
        "input": grad_tokens,
        "end_down": finish_down,
        "end_up": finish_up,
        "end_qkv": finish_qkv,
    }
    for item in ORDER:
        if item in work:
            work[item]()
        elif chunked:
            add(item)
    if chunked:
        gain2, bias2, down_b, gain1, bias1, out_b, query_b, value_b, up_b = kept["vec"]
    else:
        sums1, sums0 = kept["sums1"], whole_rows(lax.axis_index("stream"), kept["sums", 0], kept["sums", 1])
        each = [sums2[0], sums2[1], sums2[2], sums1[0], sums1[1], sums1[2], sums0[0], sums0[1], sums_up[0]]
        each = [lax.psum(lax.psum_scatter(x, "batch", scatter_dimension=0, tiled=True), "stream") for x in each]
        gain2, bias2, down_b, gain1, bias1, out_b, query_b, value_b, up_b = each
    return (
        loss.reshape(()),
        hidden_out.reshape(tokens.shape),
        kept["input"].reshape(tokens.shape),
        kept["g_q"],
        query_b,
        kept["g_k"],
        kept["g_v"],
        value_b,
        kept["g_o"],
        out_b,
        gain1,
        bias1,
        kept["g_up"],
        up_b,
        kept["g_down"],
        down_b,
        gain2,
        bias2,
    )


def solution(mesh):
    batches = mesh.shape["batch"]
    held = P("stream", "batch", None)
    split, rows = P("batch"), P("batch", None)
    return jax.shard_map(
        functools.partial(local, batches),
        mesh=mesh,
        in_specs=(held, held) + (P(),) * 16,
        out_specs=(P(), held, held, rows, split, rows, rows, split, rows, split, split, split, rows, split, rows, split, split, split),
        check_vma=False,
    )
```

```python
import functools

import jax
import jax.numpy as jnp
import numpy as np
from jax import lax
from jax.experimental import pallas as pl
from jax.experimental.pallas import tpu as pltpu
from jax.sharding import PartitionSpec as P

D = 768
HEADS = 12
HD = 64
LEN = 512
SEGS = 4
FF = 3072
HALF = D // 2
FH = FF // 2
PAIRS = HEADS // 2
ROWS8 = 8
MIB = 1 << 20
AXES = ("stream", "batch")
BF = jnp.bfloat16
F32 = jnp.float32
EPS = 1e-06
LOG2E = 1.4426950408889634
VECTORS = 16
COST_RATE = 1.15e9
COSTS = {"loss": 3.0, "hidden": 3.5, "down": 60.0, "first": 60.0, "up": 0.1, "heads0": 0.1, "heads1": 30.0, "qkv": 0.1, "input": 0.1, "add": 3.0, "end": 0.6}
PLANS = {
    "a": ("xwyz", "xzyw"),
    "b": ("xzyw", "zyxw"),
    "u": ("yxwz", "zxyw"),
    "q": ("zyxw", "zxyw"),
    "r": ("xyzw", "yxwz"),
}
ORDER = ("down", "first", "up", "heads0", "heads1", *"abu", "qkv", "input", *"abuqrabuqrabuqr", "end_down", "q", "end_up", "r", "end_qkv")


def shape_of(shape, dtype):
    return jax.ShapeDtypeStruct(tuple(shape), dtype)


def cost(micros):
    return pl.CostEstimate(flops=int(micros * COST_RATE) + 1, bytes_accessed=0, transcendentals=0)


class Pieces:
    def __init__(self, ref, places):
        self.refs, self.places = [ref] * len(places), places

    def get(self, i=0):
        return window(self.refs[i], self.places[i])


def near(x):
    return ("near", x)


def after(*arrays):
    return [("after", x) for x in arrays]


def late(x, *places):
    return ("late", x, places or ((),))


def window(ref, index):
    return ref.at[index] if index != () else ref


def call(body, outs, args, name, micros, limit=8, scratch=()):
    spaces = {"near": pltpu.VMEM, "after": pl.ANY, "late": pltpu.VMEM}

    def whole(*refs):
        ins, rest = refs[: len(args)], refs[len(args) :]
        operands = []
        for arg, ref in zip(args, ins):
            if arg[0] == "late":
                operands.append(Pieces(ref, [x() if callable(x) else x for x in arg[2]]))
            elif arg[0] != "after":
                operands.append(ref)
        body(*operands, *rest)

    return pl.pallas_call(
        whole,
        out_shape=outs,
        in_specs=[pl.BlockSpec(memory_space=spaces[arg[0]]) for arg in args],
        out_specs=[pl.BlockSpec(memory_space=pltpu.VMEM)] * len(outs),
        scratch_shapes=list(scratch),
        compiler_params=pltpu.CompilerParams(vmem_limit_bytes=limit * MIB),
        cost_estimate=cost(micros),
        name=name,
    )(*[arg[1] for arg in args])


def lanes_of(start, width):
    return (slice(None), slice(start, start + width))


def dot(left, right):
    return jnp.dot(left, right, preferred_element_type=F32)


def dot_nt(left, right):
    return lax.dot_general(left, right, (((1,), (1,)), ((), ())), preferred_element_type=F32)


def dot_tn(left, right):
    return lax.dot_general(left, right, (((0,), (0,)), ((), ())), preferred_element_type=F32)


def wide(ref):
    return ref[...].astype(F32)


FIRST, MIXED, TOKENS, STACK = 0, D, 2 * D, 3 * D


def normalize(x):
    center = jnp.mean(x, axis=-1, keepdims=True)
    offset = x - center
    spread = jnp.mean(offset * offset, axis=-1, keepdims=True)
    scale = lax.rsqrt(spread + EPS)
    return offset * scale, scale


def thirds(x):
    high = x.astype(BF).astype(F32)
    middle = (x - high).astype(BF).astype(F32)
    return high, middle, x - high - middle


def lane(ref):
    return ref[...].astype(F32).reshape(1, -1)


def segment_counts(seg_row, seg):
    return jnp.sum((seg_row == seg).astype(F32), axis=-1, keepdims=True)


def column_of(seg_row):
    return jnp.broadcast_to(seg_row.astype(F32), (128, LEN)).T[:, :1].astype(jnp.int32)


def forward_body(
    tok_h, seg, qw_h, kw_h, vw_h, ow_h, uw_h, dw_h, qb, vb, ob, gain1, shift1, ub, db, gain2, shift2,
    embeds, scale1, out_h, act_h, stack_h, q_h, k_h, v_h, p_h, slope_h, normed1_h, tail_h,
    qw, kw, vw, ow, uw, dw, out, act, stack, q, k, v, p, slope, normed1, tail, bias, kept, sems,
):
    tokens = stack.at[:, TOKENS:STACK]
    loads = [
        pltpu.make_async_copy(src, dst, sems.at[i])
        for i, (src, dst) in enumerate(
            ((tok_h, tokens), (qw_h, qw), (kw_h, kw), (vw_h, vw), (ow_h, ow), (uw_h, uw), (dw_h, dw))
        )
    ]
    for load in loads[:4]:
        load.start()
    stores = []

    def store(source, home):
        copy = pltpu.make_async_copy(source, home, sems.at[len(loads) + len(stores)])
        copy.start()
        stores.append(copy)

    owner = column_of(seg[...])
    bias[...] = jnp.where(owner == seg[...], 0.0, -1e30)
    loads[0].wait()
    x = stack[:, TOKENS:STACK]
    for weight, load, shift, ref, home in (
        (qw, loads[1], qb, q, q_h), (kw, loads[2], None, k, k_h), (vw, loads[3], vb, v, v_h)
    ):
        load.wait()
        y = dot(x, weight[...])
        ref[...] = (y if shift is None else y + lane(shift)).astype(BF)
        store(ref, home)

    for load in loads[4:]:
        load.start()
    first_rows = lax.broadcasted_iota(jnp.int32, (LEN, 2 * HD), 1) < HD

    def pair(i, carry):
        lanes = pl.ds(pl.multiple_of(i * 2 * HD, 2 * HD), 2 * HD)
        q2, k2 = q[:, lanes], k[:, lanes]
        turned = v[:, lanes].T
        zero = jnp.zeros_like(q2)
        parts = []
        for half in range(2):
            keep = first_rows if half == 0 else jnp.logical_not(first_rows)
            scores = dot_nt(jnp.where(keep, k2, zero), q2) + bias[...]
            peak = jnp.max(scores, axis=0, keepdims=True)
            expo = jnp.exp2((scores - peak) * (0.125 * LOG2E))
            total = jnp.sum(expo, axis=0, keepdims=True)
            probs = (expo * (1.0 / total)).astype(BF)
            p[2 * i + half] = probs
            parts.append(dot(turned[half * HD : (half + 1) * HD], probs))
        mixed = jnp.concatenate(parts, axis=0).T.astype(BF)
        stack[:, pl.ds(pl.multiple_of(MIXED + i * 2 * HD, 2 * HD), 2 * HD)] = mixed
        return carry

    for i in range(PAIRS):
        pair(i, 0)
    store(p, p_h)
    loads[4].wait()
    x = stack[:, TOKENS:STACK].astype(F32) + dot(stack[:, MIXED:TOKENS], ow[...]) + lane(ob)
    n, s = normalize(x)
    normed1[...] = n.astype(BF)
    store(normed1, normed1_h)
    scale1[...] = s
    kept[...] = n * lane(gain1) + lane(shift1)
    stack[:, FIRST:MIXED] = kept[...].astype(BF)
    store(stack, stack_h)
    loads[5].wait()
    loads[6].wait()
    low = stack[:, FIRST:MIXED]
    total = None
    for start in range(0, FF, D):
        cols = slice(start, start + D)
        hidden = dot(low, uw[:, cols]) + ub[cols].astype(F32).reshape(1, -1)
        phi = 0.5 * (1.0 + lax.erf(hidden * 0.7071067811865476))
        low_act = (hidden * phi).astype(BF)
        act[:, cols] = low_act
        density = jnp.exp2(hidden * hidden * (-0.5 * LOG2E)) * 0.3989422804014327
        slope[:, cols] = (phi + hidden * density).astype(BF)
        store(act.at[:, cols], act_h.at[:, cols])
        store(slope.at[:, cols], slope_h.at[:, cols])
        part = dot(low_act, dw[cols, :])
        total = part if total is None else total + part
    n, s = normalize(kept[...] + total + lane(db))
    tail[:LEN, :D] = n.astype(BF)
    slot = lax.broadcasted_iota(jnp.int32, (LEN, 128), 1)
    high, middle, low_part = thirds(s)
    tail[:LEN, D:] = jnp.where(slot == 0, high, jnp.where(slot == 1, middle, jnp.where(slot == 2, low_part, 0.0))).astype(BF)
    store(tail.at[:LEN], tail_h.at[:LEN])
    second = n * lane(gain2) + lane(shift2)
    out[...] = second.astype(BF)
    store(out, out_h)
    rows = lax.broadcasted_iota(jnp.int32, (ROWS8, D), 0)
    pooled = jnp.zeros((ROWS8, D), F32)
    for text in range(SEGS):
        mean = jnp.sum(jnp.where(owner == text, second, 0.0), axis=0, keepdims=True) / segment_counts(seg[...], text)
        pooled = jnp.where(rows == text, mean, pooled)
    for i, part in enumerate(thirds(pooled)):
        rows16 = slice(LEN + 16 * i, LEN + 16 * i + 16)
        tail[rows16, :D] = jnp.concatenate([part, jnp.zeros_like(part)], axis=0).astype(BF)
        tail[rows16, D:] = jnp.zeros((16, 128), BF)
    store(tail.at[LEN:], tail_h.at[LEN:])
    embed = (pooled * lax.rsqrt(jnp.sum(pooled * pooled, axis=-1, keepdims=True) + EPS)).astype(BF)[:SEGS]
    for i in range(embeds.shape[0]):
        embeds[i] = embed
    for copy in stores:
        copy.wait()


def forward(devices, tok, seg, weights, vectors):
    here, away = pl.BlockSpec(memory_space=pltpu.VMEM), pl.BlockSpec(memory_space=pltpu.HBM)
    low, full, square = ((LEN, D), BF), ((LEN, D), F32), ((D, D), BF)
    outs = [((devices, SEGS, D), BF), ((LEN, 1), F32)]
    saved = [low, ((LEN, FF), BF), ((LEN, STACK), BF), low, low, low, ((HEADS, LEN, LEN), BF), ((LEN, FF), BF), low, ((LEN + 48, D + 128), BF)]
    scratch = [square] * 4 + [((D, FF), BF), ((FF, D), BF)] + saved + [((LEN, LEN), F32), full]
    return pl.pallas_call(
        forward_body,
        out_shape=[shape_of(*x) for x in outs + saved],
        in_specs=[away, here] + [away] * 6 + [here] * 9,
        out_specs=[here] * len(outs) + [away] * len(saved),
        scratch_shapes=[pltpu.VMEM(*x) for x in scratch] + [pltpu.SemaphoreType.DMA((7 + len(saved) + 7,))],
        compiler_params=pltpu.CompilerParams(vmem_limit_bytes=56 * MIB),
        cost_estimate=cost(25.0),
        name="forward",
    )(tok, seg, *weights, *vectors)


def half_of(ref, index, width):
    return ref[:, pl.ds(pl.multiple_of(index * width, 128), width)]


def norm_back(grad_out, gain, normed, scale):
    weighted = grad_out * gain
    mean_plain = jnp.mean(weighted, axis=-1, keepdims=True)
    mean_cross = jnp.mean(weighted * normed, axis=-1, keepdims=True)
    return scale * (weighted - mean_plain - normed * mean_cross)


def column_sum(x):
    return jnp.sum(x.astype(F32), axis=0, keepdims=True)


def loss_body(texts, tail, gathered, pos, seg, gain, loss, branch, branch_send, sums, tall):
    stream, batch = lax.axis_index("stream"), lax.axis_index("batch")
    for i in range(gathered.shape[0]):
        tall[i, :SEGS] = gathered[i].astype(F32)
        tall[i, SEGS:] = jnp.zeros((ROWS8 - SEGS, D), F32)
    every = tall[...].reshape(4 * texts, D).astype(BF)
    span = 2 * texts
    row = lax.broadcasted_iota(jnp.int32, (texts, span), 0)
    col = lax.broadcasted_iota(jnp.int32, (texts, span), 1)
    pick = (col == (row // SEGS) * ROWS8 + row % SEGS).astype(F32).astype(BF)
    query = dot(pick, every[:span]).astype(BF)
    passage = dot(pick, every[span:]).astype(BF)
    scores = dot_nt(passage, query) * 100.0
    peak = jnp.max(scores, axis=0, keepdims=True)
    log_total = peak + jnp.log(jnp.sum(jnp.exp(scores - peak), axis=0, keepdims=True))
    chosen = (lax.broadcasted_iota(jnp.int32, (texts, texts), 0) == pos[...]).astype(F32)
    losses = log_total - jnp.sum(chosen * scores, axis=0, keepdims=True)
    loss[...] = jnp.sum(losses, axis=1, keepdims=True) / texts
    grad_scores = ((jnp.exp(scores - log_total) - chosen) / texts).astype(BF)
    row = lax.broadcasted_iota(jnp.int32, (ROWS8, texts), 0)
    col = lax.broadcasted_iota(jnp.int32, (ROWS8, texts), 1)
    mine = jnp.logical_and(col == batch * SEGS + row, row < SEGS).astype(F32).astype(BF)
    to_query = dot(dot_nt(mine, grad_scores).astype(BF), passage)
    to_passage = dot(dot(mine, grad_scores).astype(BF), query)
    grad_embed = jnp.where(stream == 0, to_query, to_passage) * 100.0
    pooled = sum(tail[LEN + 16 * i : LEN + 16 * i + 16, :D].astype(F32) for i in range(3))[:ROWS8]
    inverse = lax.rsqrt(jnp.sum(pooled * pooled, axis=-1, keepdims=True) + EPS)
    cross = jnp.sum(grad_embed * pooled, axis=-1, keepdims=True)
    grad_pooled = inverse * grad_embed - pooled * (inverse * inverse * inverse * cross)
    owner = column_of(seg[...])
    grad_second = jnp.zeros((LEN, D), F32)
    for text in range(SEGS):
        share = grad_pooled[text : text + 1] / segment_counts(seg[...], text)
        grad_second = jnp.where(owner == text, share, grad_second)
    n = tail[:LEN, :D].astype(F32)
    scale = sum(tail[:LEN, D:].astype(F32)[:, i : i + 1] for i in range(3))
    resid = norm_back(grad_second, lane(gain), n, scale)
    branch[...] = resid.astype(BF)
    branch_send[...] = half_of(branch, 1 - stream, HALF)
    sums[0:1] = column_sum(grad_second * n)
    sums[1:2] = column_sum(grad_second)
    sums[2:3] = column_sum(branch[...])


def hidden_body(dw, slope, branch, grad_hidden, send, sums):
    for j in range(len(dw.refs)):
        cols = slice(j * D, (j + 1) * D)
        grad = (dot_nt(branch[...], dw.get(j)[...]) * slope.get(j)[...].astype(F32)).astype(BF)
        grad_hidden[:, cols] = grad
        sums[:, cols] = column_sum(grad)
    send[...] = half_of(grad_hidden, 1 - lax.axis_index("stream"), FH)


def where_to(plan, i):
    stream, relative = lax.axis_index("stream"), lax.axis_index("batch") ^ i
    slots = []
    for bits in plan:
        last = len(bits) - 1
        slots.append(sum((((relative >> bit) & 1) << (last - step)) for step, bit in enumerate(bits)))
    return jnp.where(stream == 0, slots[0], slots[1])


def put_chunk(part, slot, keep, send, lanes):
    here = keep.shape[0]

    @pl.when(slot < here)
    def _():
        keep[slot, :, lanes] = part

    @pl.when(slot >= here)
    def _():
        send[slot - here, :, lanes] = part


def place_rows(total, first, rows, groups, outs, start):
    if groups is None:
        outs[0][first : first + total.shape[0], start : start + total.shape[1]] = total
        return
    low = total.astype(BF)
    for n, (plan, top, height, left, width) in enumerate(groups):
        begin, end = max(left, start), min(left + width, start + total.shape[1])
        if begin >= end:
            continue
        for i in range(total.shape[0] // rows):
            piece = low[i * rows + top : i * rows + top + height, begin - start : end - start]
            put_chunk(piece, where_to(plan, first // rows + i), outs[2 * n], outs[2 * n + 1], slice(begin - left, end - left))


def outer_body(rows, groups, counts, left, left_other, *refs):
    rights, outs = refs[: 2 * len(counts)], refs[2 * len(counts) :]
    start = piece = 0
    for i, count in enumerate(counts):
        right, right_other = rights[2 * i : 2 * i + 2]
        columns = right_other.shape[1]
        mine = right[...] if right.shape[1] == columns else half_of(right, lax.axis_index("stream"), columns)
        other = right_other[...]
        for j in range(count):
            total = dot_tn(left.get(piece)[...], mine) + dot_tn(left_other.get(piece)[...], other)
            piece += 1
            place_rows(total, j * D, rows, groups, outs, start)
        start += columns


def first_body(uw, normed, scale, grad_hidden, branch, gain, attn, sums):
    grad_first = branch[...].astype(F32)
    for j in range(len(uw.refs)):
        grad_first += dot_nt(grad_hidden[:, j * D : (j + 1) * D], uw.get(j)[...])
    n = normed.get()[...].astype(F32)
    resid = norm_back(grad_first, lane(gain), n, scale.get()[...])
    attn[...] = resid.astype(BF)
    sums[0:1] = column_sum(grad_first * n)
    sums[1:2] = column_sum(grad_first)
    sums[2:3] = column_sum(attn[...])


def half_index(which):
    stream = lax.axis_index("stream")
    return stream if which else 1 - stream


def head_lanes(which):
    return lambda: (slice(None), pl.ds(pl.multiple_of(half_index(which) * HALF, 128), HALF))


def head_rows(which):
    return lambda: pl.ds(pl.multiple_of(half_index(which) * HALF, 128), HALF)


def head_pair(which, i):
    return lambda: pl.ds(half_index(which) * (HEADS // 2) + 2 * i, 2)


def attend_back_body(which, ow, v, k, q, p, attn, grads_qk, grads_v, sums):
    grad_mixed = dot_nt(attn[...], ow.get()[...]).astype(BF)
    first_lanes = lax.broadcasted_iota(jnp.int32, (LEN, 2 * HD), 1) < HD
    for i in range(PAIRS // 2):
        lanes = slice(i * 2 * HD, (i + 1) * 2 * HD)
        g2, v2, k2, q2 = grad_mixed[:, lanes], v.get()[:, lanes], k.get()[:, lanes], q.get()[:, lanes]
        zero = jnp.zeros_like(q2)
        turned = k2.T
        tq, tk, tv = [], None, None
        for half in range(2):
            keep = first_lanes if half == 0 else jnp.logical_not(first_lanes)
            probs = p.get(i)[half]
            g = jnp.where(keep, g2, zero)
            weighted = dot_nt(v2, g) * probs.astype(F32)
            inner = jnp.sum(weighted, axis=0, keepdims=True)
            raw = (weighted - probs.astype(F32) * inner).astype(BF)
            tq.append(dot(turned[half * HD : (half + 1) * HD], raw))
            parts = (dot(raw, jnp.where(keep, q2, zero)), dot(probs, g))
            tk, tv = parts if half == 0 else (tk + parts[0], tv + parts[1])
        for j, grad in enumerate((jnp.concatenate(tq, axis=0).T * 0.125, tk * 0.125, tv)):
            ref, start = (grads_v, i * 2 * HD) if j == 2 else (grads_qk, j * HALF + i * 2 * HD)
            ref[:, start : start + 2 * HD] = grad.astype(BF)
    grads_v[:, HALF:] = half_of(attn, half_index(which), HALF)
    sums[0:1] = column_sum(grads_qk[:, :HALF])
    sums[1:2] = column_sum(grads_v[:, :HALF])


VEC = ("gain2", "bias2", "down", "gain1", "bias1", "out", "query", "value")


def whole_rows(stream, away, own):
    return jnp.where(stream == 0, jnp.concatenate([own, away], axis=1), jnp.concatenate([away, own], axis=1))


def qkv_outer_body(rows, groups, left, left_other, *refs):
    rights, (sums2, sums1, sums_away, sums_own, sums_up), outs = refs[:4], refs[4:9], refs[9:]
    if groups is not None:
        plan, _, _, first_lane, _ = groups[-1]
        blank = jnp.zeros((128 - len(VEC), D), F32)
        sums0 = whole_rows(lax.axis_index("stream"), sums_away[0:2], sums_own[0:2])
        turned = jnp.concatenate([sums2[0:3], sums1[0:3], sums0, blank], axis=0).T
        tall = jnp.broadcast_to(sums_up[...], (128, FF)).T.reshape(D // rows, FF // D, rows, 128)
        slot = lax.broadcasted_iota(jnp.int32, (rows, 128), 1)
        for i in range(D // rows):
            piece = turned[i * rows : (i + 1) * rows]
            for part in range(FF // D):
                piece = jnp.where(slot == len(VEC) + part, tall[i, part], piece)
            lanes = slice(4 * HALF - first_lane, 4 * HALF - first_lane + 128)
            put_chunk(piece.astype(BF), where_to(plan, i), outs[-2], outs[-1], lanes)
    own_qk, own_v, other_qk, other_v = rights
    start = 0
    for i, (own, other) in enumerate(((own_qk, other_qk), (own_v, other_v))):
        for j in range(2):
            lanes, piece = slice(j * HALF, (j + 1) * HALF), i * j
            total = dot_tn(left.get(piece)[...], own[:, lanes]) + dot_tn(left_other.get(piece)[...], other[:, lanes])
            place_rows(total, 0, rows, groups, outs, start)
            start += HALF


def input_body(qw, kw, vw, attn, *refs):
    out = refs[-1]
    total = attn[...].astype(F32)
    for i, weight in enumerate((qw, kw, vw)):
        for which in range(2):
            grads = refs[2 * which + i // 2][:, i % 2 * HALF : (i % 2 + 1) * HALF]
            total += dot_nt(grads, weight.get(which)[...])
    out[...] = total


def add_body(keep, arrived, *outs):
    if len(outs) == 1:
        outs[0][...] = (wide(keep) + wide(arrived)).astype(BF)
        return
    half = outs[0].shape[0]
    outs[0][...] = (keep[:half].astype(F32) + arrived[:half].astype(F32)).astype(BF)
    outs[1][...] = (keep[half:].astype(F32) + arrived[half:].astype(F32)).astype(BF)


def final_body(count, pieces, vectors, *refs):
    mine, other, outs = refs[:count], refs[count : 2 * count], refs[2 * count :]
    swap = lax.axis_index("stream") != 0
    for ref, parts in zip(outs, pieces):
        middle = ref.shape[1] // 2
        at = {}
        for which, lane_from, lanes, top in parts:
            a, b = mine[which][:, lane_from : lane_from + lanes], other[which][:, lane_from : lane_from + lanes]
            rows, begin = slice(top, top + a.shape[0]), at.get(top, 0)
            ref[rows, begin : begin + lanes] = jnp.where(swap, b, a).astype(F32)
            ref[rows, middle + begin : middle + begin + lanes] = jnp.where(swap, a, b).astype(F32)
            at[top] = begin + lanes
    if vectors is not None:
        both = (mine[-1][:, vectors:].astype(F32) + other[-1][:, vectors:].astype(F32)).T
        for i, ref in enumerate(outs[len(pieces) :]):
            if i < len(VEC):
                ref[...] = both[i]
            else:
                ref[...] = jnp.concatenate([both[i + j : i + j + 1] for j in range(FF // D)], axis=1).reshape(-1)


def swap_cores(x):
    return lax.ppermute(x, "stream", [(0, 1), (1, 0)])


AXIS_BITS = {"x": 0, "y": 1, "z": 2, "w": 3}


def bit_plan(plan, batches):
    count = batches.bit_length() - 1
    return [[AXIS_BITS[axis] for axis in order] if count == len(order) else list(range(count)) for order in plan]


def halve_send(send, plan, batches, step):
    pairs = [
        (core * batches + b, core * batches + (b ^ (1 << plan[core][step]))) for core in range(2) for b in range(batches)
    ]
    return lax.ppermute(send, AXES, pairs)


def local(
    batches,
    tokens,
    seg_ids,
    pos_ids,
    q_weight,
    q_bias,
    k_weight,
    v_weight,
    v_bias,
    o_weight,
    o_bias,
    norm1_gain,
    norm1_bias,
    up_weight,
    up_bias,
    down_weight,
    down_bias,
    norm2_gain,
    norm2_bias,
):
    texts = pos_ids.shape[0]
    rows = D // batches
    chunked = rows % 16 == 0 and batches & (batches - 1) == 0
    stages = batches.bit_length() - 1
    tok, seg, pos = tokens.reshape(LEN, D), seg_ids.reshape(1, LEN), pos_ids.reshape(1, texts)
    low, sums = shape_of((LEN, D), BF), shape_of((ROWS8, D), F32)
    low_half = shape_of((LEN, HALF), BF)
    wide_low = shape_of((LEN, FF), BF)
    tall = FF // batches
    cuts = {
        "a": ("down", 0, tall // 2, 0, HALF),
        "b": ("down", tall // 2, tall // 2, 0, HALF),
        "u": ("up", 0, rows, 0, FH),
        "q": ("qkv", 0, rows, 0, 2 * HALF),
        "r": ("qkv", 0, rows, 2 * HALF, 2 * HALF + 128),
    }
    plans = {name: bit_plan(plan, batches) for name, plan in PLANS.items()}
    token = []

    def run(body, outs, args, name, micros, limit=8, **more):
        results = call(body, outs, args + after(*token), name, micros, limit if chunked else 48, **more)
        token[:] = [results[0]]
        return results

    embeds, scale1, hidden_out, act, stack, q, k, v, p, slope, normed1, tail = forward(
        2 * batches,
        tok,
        seg,
        (q_weight, k_weight, v_weight, o_weight, up_weight, down_weight),
        (q_bias, v_bias, o_bias, norm1_gain, norm1_bias, up_bias, down_bias, norm2_gain, norm2_bias),
    )
    gathered = lax.all_to_all(embeds, AXES, split_axis=0, concat_axis=0)
    act_other = swap_cores(act)
    stack_other = swap_cores(stack)
    loss, branch, branch_send, sums2 = run(
        functools.partial(loss_body, texts),
        [shape_of((1, 1), F32), low, low_half, sums],
        [near(tail), near(gathered), near(pos), near(seg), near(norm2_gain)],
        "loss",
        COSTS["loss"],
        scratch=[pltpu.VMEM((2 * batches, ROWS8, D), F32)],
    )
    branch_other = swap_cores(branch_send)
    grad_hidden, hidden_send, sums_up = run(
        hidden_body,
        [wide_low, shape_of((LEN, FH), BF), shape_of((1, FF), F32)],
        [
            late(down_weight, *[(slice(j, j + D), slice(None)) for j in range(0, FF, D)]),
            late(slope, *[lanes_of(j, D) for j in range(0, FF, D)]),
            near(branch),
        ],
        "hidden",
        COSTS["hidden"],
    )
    hidden_other = swap_cores(hidden_send)
    held, arriving, step_of, kept = {}, {}, {}, {}

    def send(name):
        if step_of[name] < stages:
            arriving[name] = halve_send(held[name][-1], plans[name], batches, step_of[name])
        else:
            arriving[name] = swap_cores(held[name][0][0])

    def add(name):
        keep, arrived = held[name][0], arriving[name]
        count = keep.shape[0]
        sizes = [count // 2] * 2 if count > 1 else [1]
        outs = [shape_of((size,) + keep.shape[1:], BF) for size in sizes]
        step_of[name] += 1
        held[name] = run(add_body, outs, [near(keep), near(arrived)], f"{name}_add{step_of[name]}", COSTS["add"])
        send(name)

    def outer(product, body, size, columns, own, other, starts, rights, others=()):
        windows = [lanes_of(start, D) for start in starts]
        args = [late(own, *windows), late(other, *windows)] + [near(x) for x in rights] + [near(x) for x in others]
        height = size // batches
        if not chunked:
            outs = [shape_of((size, columns), F32)]
            kept[product] = run(functools.partial(body, height, None), outs, args, f"outer_{product}", COSTS[product], 12)[0]
            return
        names = [name for name, cut in cuts.items() if cut[0] == product]
        groups = [(plans[name],) + cuts[name][1:] for name in names]
        outs = [shape_of((batches // 2, cuts[name][2], cuts[name][4]), BF) for name in names for _ in range(2)]
        results = run(functools.partial(body, height, groups), outs, args, f"outer_{product}", COSTS[product], 12)
        for i, name in enumerate(names):
            held[name], step_of[name] = results[2 * i : 2 * i + 2], 0
            send(name)

    def plain(*counts):
        return lambda height, groups, *refs: outer_body(height, groups, counts, *refs)

    def down():
        outer("down", plain(FF // D), FF, HALF, act, act_other, range(0, FF, D), [branch, branch_other])

    def first():
        kept["attn"], kept["sums1"] = run(
            first_body,
            [low, sums],
            [
                late(up_weight, *[lanes_of(j, D) for j in range(0, FF, D)]),
                late(normed1),
                late(scale1),
                near(grad_hidden),
                near(branch),
                near(norm1_gain),
            ],
            "first",
            COSTS["first"],
        )

    def up():
        outer("up", plain(1), D, FH, stack, stack_other, (FIRST,), [grad_hidden, hidden_other])

    def heads(which):
        lanes = head_lanes(which)
        *kept["grads", which], kept["sums", which] = run(
            functools.partial(attend_back_body, which),
            [low, low, shape_of((ROWS8, HALF), F32)],
            [
                late(o_weight, head_rows(which)),
                late(v, lanes),
                late(k, lanes),
                late(q, lanes),
                late(p, *[head_pair(which, i) for i in range(PAIRS // 2)]),
                near(kept["attn"]),
            ],
            f"attend_back{which}",
            COSTS[f"heads{which}"],
            10,
        )
        if which == 0:
            kept["grads_other"] = [swap_cores(x) for x in kept["grads", 0]]

    def qkv():
        vectors = [sums2, kept["sums1"], kept["sums", 0], kept["sums", 1], sums_up]
        columns = 4 * HALF + (128 if chunked else 0)
        rights = kept["grads", 1] + kept["grads_other"]
        outer("qkv", qkv_outer_body, D, columns, stack, stack_other, (TOKENS, MIXED), rights, vectors)

    def grad_tokens():
        weights = [late(w, head_lanes(0), head_lanes(1)) for w in (q_weight, k_weight, v_weight)]
        grads = [near(x) for x in [kept["attn"]] + kept["grads", 0] + kept["grads", 1]]
        kept["input"] = run(input_body, [shape_of((LEN, D), F32)], weights + grads, "input", COSTS["input"])[0]

    def finish(product, names, pieces, vectors=None):
        if chunked:
            mine, other = [held[name][0][0] for name in names], [arriving[name] for name in names]
        else:
            share = lax.psum_scatter(kept[product], "batch", scatter_dimension=0, tiled=True).astype(BF)
            mine, other = [share], [swap_cores(share)]
        height = (FF if product == "down" else D) // batches
        outs = [shape_of((height, 2 * sum(x[2] for x in parts if x[3] == 0)), F32) for parts in pieces]
        if vectors is not None:
            outs += [shape_of((rows,), F32)] * len(VEC) + [shape_of((tall,), F32)]
        args = [near(x) for x in mine + other]
        return run(functools.partial(final_body, len(mine), pieces, vectors), outs, args, f"final_{names[-1]}", COSTS["end"])

    def finish_down():
        pieces = [(0, 0, HALF, 0), (1, 0, HALF, tall // 2)] if chunked else [(0, 0, HALF, 0)]
        kept["g_down"] = finish("down", "ab", [pieces])[0]

    def finish_up():
        kept["g_up"] = finish("up", "u", [[(0, 0, FH, 0)]])[0]

    def finish_qkv():
        where = ((0, 0), (0, HALF), (1, 0), (1, HALF)) if chunked else [(0, i * HALF) for i in range(4)]
        pieces = [[(which, start, HALF, 0)] for which, start in where]
        results = finish("qkv", "qr", pieces, 2 * HALF if chunked else None)
        kept["g_q"], kept["g_k"], kept["g_v"], kept["g_o"], *kept["vec"] = results

    work = {
        "down": down,
        "first": first,
        "up": up,
        "heads0": lambda: heads(0),
        "heads1": lambda: heads(1),
        "qkv": qkv,
        "input": grad_tokens,
        "end_down": finish_down,
        "end_up": finish_up,
        "end_qkv": finish_qkv,
    }
    for item in ORDER:
        if item in work:
            work[item]()
        elif chunked:
            add(item)
    if chunked:
        gain2, bias2, down_b, gain1, bias1, out_b, query_b, value_b, up_b = kept["vec"]
    else:
        sums1, sums0 = kept["sums1"], whole_rows(lax.axis_index("stream"), kept["sums", 0], kept["sums", 1])
        each = [sums2[0], sums2[1], sums2[2], sums1[0], sums1[1], sums1[2], sums0[0], sums0[1], sums_up[0]]
        each = [lax.psum(lax.psum_scatter(x, "batch", scatter_dimension=0, tiled=True), "stream") for x in each]
        gain2, bias2, down_b, gain1, bias1, out_b, query_b, value_b, up_b = each
    return (
        loss.reshape(()),
        hidden_out.reshape(tokens.shape),
        kept["input"].reshape(tokens.shape),
        kept["g_q"],
        query_b,
        kept["g_k"],
        kept["g_v"],
        value_b,
        kept["g_o"],
        out_b,
        gain1,
        bias1,
        kept["g_up"],
        up_b,
        kept["g_down"],
        down_b,
        gain2,
        bias2,
    )


def solution(mesh):
    batches = mesh.shape["batch"]
    held = P("stream", "batch", None)
    split, rows = P("batch"), P("batch", None)
    return jax.shard_map(
        functools.partial(local, batches),
        mesh=mesh,
        in_specs=(held, held) + (P(),) * 16,
        out_specs=(P(), held, held, rows, split, rows, rows, split, rows, split, split, split, rows, split, rows, split, split, split),
        check_vma=False,
    )
```

```python
import functools

import jax
import jax.numpy as jnp
import numpy as np
from jax import lax
from jax.experimental import pallas as pl
from jax.experimental.pallas import tpu as pltpu
from jax.sharding import PartitionSpec as P

D = 768
HEADS = 12
HD = 64
LEN = 512
SEGS = 4
FF = 3072
HALF = D // 2
FH = FF // 2
PAIRS = HEADS // 2
ROWS8 = 8
MIB = 1 << 20
AXES = ("stream", "batch")
BF = jnp.bfloat16
F32 = jnp.float32
EPS = 1e-06
LOG2E = 1.4426950408889634
VECTORS = 16
COST_RATE = 1.15e9
COSTS = {"loss": 3.0, "hidden": 3.5, "down": 60.0, "first": 60.0, "up": 0.1, "heads0": 0.1, "heads1": 30.0, "qkv": 0.1, "input": 0.1, "add": 3.0, "end": 0.6}
PLANS = {
    "a": ("xwyz", "zxyw"),
    "b": ("ywxz", "yzxw"),
    "u": ("xwyz", "zyxw"),
    "q": ("xyzw", "zxyw"),
    "r": ("xzyw", "yxwz"),
}
ORDER = ("down", "first", "up", "heads0", *"ab", "heads1", "vectors", "qkv", "input", *"uabqruabqruabq", *"ru", "end_down", "q", "r", "end_up", "end_qkv")


def shape_of(shape, dtype):
    return jax.ShapeDtypeStruct(tuple(shape), dtype)


def cost(micros):
    return pl.CostEstimate(flops=int(micros * COST_RATE) + 1, bytes_accessed=0, transcendentals=0)


class Pieces:
    def __init__(self, ref, places):
        self.refs, self.places = [ref] * len(places), places

    def get(self, i=0):
        return window(self.refs[i], self.places[i])


def near(x):
    return ("near", x)


def after(*arrays):
    return [("after", x) for x in arrays]


def late(x, *places):
    return ("late", x, places or ((),))


def window(ref, index):
    return ref.at[index] if index != () else ref


def call(body, outs, args, name, micros, limit=8, scratch=()):
    spaces = {"near": pltpu.VMEM, "after": pl.ANY, "late": pltpu.VMEM}

    def whole(*refs):
        ins, rest = refs[: len(args)], refs[len(args) :]
        operands = []
        for arg, ref in zip(args, ins):
            if arg[0] == "late":
                operands.append(Pieces(ref, [x() if callable(x) else x for x in arg[2]]))
            elif arg[0] != "after":
                operands.append(ref)
        body(*operands, *rest)

    return pl.pallas_call(
        whole,
        out_shape=outs,
        in_specs=[pl.BlockSpec(memory_space=spaces[arg[0]]) for arg in args],
        out_specs=[pl.BlockSpec(memory_space=pltpu.VMEM)] * len(outs),
        scratch_shapes=list(scratch),
        compiler_params=pltpu.CompilerParams(vmem_limit_bytes=limit * MIB),
        cost_estimate=cost(micros),
        name=name,
    )(*[arg[1] for arg in args])


def lanes_of(start, width):
    return (slice(None), slice(start, start + width))


def dot(left, right):
    return jnp.dot(left, right, preferred_element_type=F32)


def dot_nt(left, right):
    return lax.dot_general(left, right, (((1,), (1,)), ((), ())), preferred_element_type=F32)


def dot_tn(left, right):
    return lax.dot_general(left, right, (((0,), (0,)), ((), ())), preferred_element_type=F32)


def wide(ref):
    return ref[...].astype(F32)


FIRST, MIXED, TOKENS, STACK = 0, D, 2 * D, 3 * D


def normalize(x):
    center = jnp.mean(x, axis=-1, keepdims=True)
    offset = x - center
    spread = jnp.mean(offset * offset, axis=-1, keepdims=True)
    scale = lax.rsqrt(spread + EPS)
    return offset * scale, scale


def thirds(x):
    high = x.astype(BF).astype(F32)
    middle = (x - high).astype(BF).astype(F32)
    return high, middle, x - high - middle


def lane(ref):
    return ref[...].astype(F32).reshape(1, -1)


def segment_counts(seg_row, seg):
    return jnp.sum((seg_row == seg).astype(F32), axis=-1, keepdims=True)


def column_of(seg_row):
    return jnp.broadcast_to(seg_row.astype(F32), (128, LEN)).T[:, :1].astype(jnp.int32)


def forward_body(
    tok_h, seg, qw_h, kw_h, vw_h, ow_h, uw_h, dw_h, qb, vb, ob, gain1, shift1, ub, db, gain2, shift2,
    embeds, scale1, out_h, act_h, stack_h, q_h, k_h, v_h, p_h, slope_h, normed1_h, tail_h,
    qw, kw, vw, ow, uw, dw, out, act, stack, q, k, v, p, slope, normed1, tail, bias, kept, sems,
):
    tokens = stack.at[:, TOKENS:STACK]
    loads = [
        pltpu.make_async_copy(src, dst, sems.at[i])
        for i, (src, dst) in enumerate(
            ((tok_h, tokens), (qw_h, qw), (kw_h, kw), (vw_h, vw), (ow_h, ow), (uw_h, uw), (dw_h, dw))
        )
    ]
    for load in loads[:4]:
        load.start()
    stores = []

    def store(source, home):
        copy = pltpu.make_async_copy(source, home, sems.at[len(loads) + len(stores)])
        copy.start()
        stores.append(copy)

    owner = column_of(seg[...])
    bias[...] = jnp.where(owner == seg[...], 0.0, -1e30)
    loads[0].wait()
    x = stack[:, TOKENS:STACK]
    for weight, load, shift, ref, home in (
        (qw, loads[1], qb, q, q_h), (kw, loads[2], None, k, k_h), (vw, loads[3], vb, v, v_h)
    ):
        load.wait()
        y = dot(x, weight[...])
        ref[...] = (y if shift is None else y + lane(shift)).astype(BF)
        store(ref, home)

    for load in loads[4:]:
        load.start()
    first_rows = lax.broadcasted_iota(jnp.int32, (LEN, 2 * HD), 1) < HD

    def pair(i, carry):
        lanes = pl.ds(pl.multiple_of(i * 2 * HD, 2 * HD), 2 * HD)
        q2, k2 = q[:, lanes], k[:, lanes]
        turned = v[:, lanes].T
        zero = jnp.zeros_like(q2)
        parts = []
        for half in range(2):
            keep = first_rows if half == 0 else jnp.logical_not(first_rows)
            scores = dot_nt(jnp.where(keep, k2, zero), q2) + bias[...]
            peak = jnp.max(scores, axis=0, keepdims=True)
            expo = jnp.exp2((scores - peak) * (0.125 * LOG2E))
            total = jnp.sum(expo, axis=0, keepdims=True)
            probs = (expo * (1.0 / total)).astype(BF)
            p[2 * i + half] = probs
            parts.append(dot(turned[half * HD : (half + 1) * HD], probs))
        mixed = jnp.concatenate(parts, axis=0).T.astype(BF)
        stack[:, pl.ds(pl.multiple_of(MIXED + i * 2 * HD, 2 * HD), 2 * HD)] = mixed
        return carry

    for i in range(PAIRS):
        pair(i, 0)
    store(p, p_h)
    loads[4].wait()
    x = stack[:, TOKENS:STACK].astype(F32) + dot(stack[:, MIXED:TOKENS], ow[...]) + lane(ob)
    n, s = normalize(x)
    normed1[...] = n.astype(BF)
    store(normed1, normed1_h)
    scale1[...] = s
    kept[...] = n * lane(gain1) + lane(shift1)
    stack[:, FIRST:MIXED] = kept[...].astype(BF)
    store(stack, stack_h)
    loads[5].wait()
    loads[6].wait()
    low = stack[:, FIRST:MIXED]
    total = None
    for start in range(0, FF, D):
        cols = slice(start, start + D)
        hidden = dot(low, uw[:, cols]) + ub[cols].astype(F32).reshape(1, -1)
        phi = 0.5 * (1.0 + lax.erf(hidden * 0.7071067811865476))
        low_act = (hidden * phi).astype(BF)
        act[:, cols] = low_act
        density = jnp.exp2(hidden * hidden * (-0.5 * LOG2E)) * 0.3989422804014327
        slope[:, cols] = (phi + hidden * density).astype(BF)
        store(act.at[:, cols], act_h.at[:, cols])
        store(slope.at[:, cols], slope_h.at[:, cols])
        part = dot(low_act, dw[cols, :])
        total = part if total is None else total + part
    n, s = normalize(kept[...] + total + lane(db))
    tail[:LEN, :D] = n.astype(BF)
    slot = lax.broadcasted_iota(jnp.int32, (LEN, 128), 1)
    high, middle, low_part = thirds(s)
    tail[:LEN, D:] = jnp.where(slot == 0, high, jnp.where(slot == 1, middle, jnp.where(slot == 2, low_part, 0.0))).astype(BF)
    store(tail.at[:LEN], tail_h.at[:LEN])
    second = n * lane(gain2) + lane(shift2)
    out[...] = second.astype(BF)
    store(out, out_h)
    rows = lax.broadcasted_iota(jnp.int32, (ROWS8, D), 0)
    pooled = jnp.zeros((ROWS8, D), F32)
    for text in range(SEGS):
        mean = jnp.sum(jnp.where(owner == text, second, 0.0), axis=0, keepdims=True) / segment_counts(seg[...], text)
        pooled = jnp.where(rows == text, mean, pooled)
    for i, part in enumerate(thirds(pooled)):
        rows16 = slice(LEN + 16 * i, LEN + 16 * i + 16)
        tail[rows16, :D] = jnp.concatenate([part, jnp.zeros_like(part)], axis=0).astype(BF)
        tail[rows16, D:] = jnp.zeros((16, 128), BF)
    store(tail.at[LEN:], tail_h.at[LEN:])
    embed = (pooled * lax.rsqrt(jnp.sum(pooled * pooled, axis=-1, keepdims=True) + EPS)).astype(BF)[:SEGS]
    for i in range(embeds.shape[0]):
        embeds[i] = embed
    for copy in stores:
        copy.wait()


def forward(devices, tok, seg, weights, vectors):
    here, away = pl.BlockSpec(memory_space=pltpu.VMEM), pl.BlockSpec(memory_space=pltpu.HBM)
    low, full, square = ((LEN, D), BF), ((LEN, D), F32), ((D, D), BF)
    outs = [((devices, SEGS, D), BF), ((LEN, 1), F32)]
    saved = [low, ((LEN, FF), BF), ((LEN, STACK), BF), low, low, low, ((HEADS, LEN, LEN), BF), ((LEN, FF), BF), low, ((LEN + 48, D + 128), BF)]
    scratch = [square] * 4 + [((D, FF), BF), ((FF, D), BF)] + saved + [((LEN, LEN), F32), full]
    return pl.pallas_call(
        forward_body,
        out_shape=[shape_of(*x) for x in outs + saved],
        in_specs=[away, here] + [away] * 6 + [here] * 9,
        out_specs=[here] * len(outs) + [away] * len(saved),
        scratch_shapes=[pltpu.VMEM(*x) for x in scratch] + [pltpu.SemaphoreType.DMA((7 + len(saved) + 7,))],
        compiler_params=pltpu.CompilerParams(vmem_limit_bytes=56 * MIB),
        cost_estimate=cost(25.0),
        name="forward",
    )(tok, seg, *weights, *vectors)


def half_of(ref, index, width):
    return ref[:, pl.ds(pl.multiple_of(index * width, 128), width)]


def norm_back(grad_out, gain, normed, scale):
    weighted = grad_out * gain
    mean_plain = jnp.mean(weighted, axis=-1, keepdims=True)
    mean_cross = jnp.mean(weighted * normed, axis=-1, keepdims=True)
    return scale * (weighted - mean_plain - normed * mean_cross)


def column_sum(x):
    return jnp.sum(x.astype(F32), axis=0, keepdims=True)


def loss_body(texts, tail, gathered, pos, seg, gain, loss, branch, branch_send, sums, tall):
    stream, batch = lax.axis_index("stream"), lax.axis_index("batch")
    for i in range(gathered.shape[0]):
        tall[i, :SEGS] = gathered[i].astype(F32)
        tall[i, SEGS:] = jnp.zeros((ROWS8 - SEGS, D), F32)
    every = tall[...].reshape(4 * texts, D).astype(BF)
    span = 2 * texts
    row = lax.broadcasted_iota(jnp.int32, (texts, span), 0)
    col = lax.broadcasted_iota(jnp.int32, (texts, span), 1)
    pick = (col == (row // SEGS) * ROWS8 + row % SEGS).astype(F32).astype(BF)
    query = dot(pick, every[:span]).astype(BF)
    passage = dot(pick, every[span:]).astype(BF)
    scores = dot_nt(passage, query) * 100.0
    peak = jnp.max(scores, axis=0, keepdims=True)
    log_total = peak + jnp.log(jnp.sum(jnp.exp(scores - peak), axis=0, keepdims=True))
    chosen = (lax.broadcasted_iota(jnp.int32, (texts, texts), 0) == pos[...]).astype(F32)
    losses = log_total - jnp.sum(chosen * scores, axis=0, keepdims=True)
    loss[...] = jnp.sum(losses, axis=1, keepdims=True) / texts
    grad_scores = ((jnp.exp(scores - log_total) - chosen) / texts).astype(BF)
    row = lax.broadcasted_iota(jnp.int32, (ROWS8, texts), 0)
    col = lax.broadcasted_iota(jnp.int32, (ROWS8, texts), 1)
    mine = jnp.logical_and(col == batch * SEGS + row, row < SEGS).astype(F32).astype(BF)
    to_query = dot(dot_nt(mine, grad_scores).astype(BF), passage)
    to_passage = dot(dot(mine, grad_scores).astype(BF), query)
    grad_embed = jnp.where(stream == 0, to_query, to_passage) * 100.0
    pooled = sum(tail[LEN + 16 * i : LEN + 16 * i + 16, :D].astype(F32) for i in range(3))[:ROWS8]
    inverse = lax.rsqrt(jnp.sum(pooled * pooled, axis=-1, keepdims=True) + EPS)
    cross = jnp.sum(grad_embed * pooled, axis=-1, keepdims=True)
    grad_pooled = inverse * grad_embed - pooled * (inverse * inverse * inverse * cross)
    owner = column_of(seg[...])
    grad_second = jnp.zeros((LEN, D), F32)
    for text in range(SEGS):
        share = grad_pooled[text : text + 1] / segment_counts(seg[...], text)
        grad_second = jnp.where(owner == text, share, grad_second)
    n = tail[:LEN, :D].astype(F32)
    scale = sum(tail[:LEN, D:].astype(F32)[:, i : i + 1] for i in range(3))
    resid = norm_back(grad_second, lane(gain), n, scale)
    branch[...] = resid.astype(BF)
    branch_send[...] = half_of(branch, 1 - stream, HALF)
    sums[0:1] = column_sum(grad_second * n)
    sums[1:2] = column_sum(grad_second)
    sums[2:3] = column_sum(branch[...])


def hidden_body(dw, slope, branch, grad_hidden, send, sums):
    for j in range(len(dw.refs)):
        cols = slice(j * D, (j + 1) * D)
        grad = (dot_nt(branch[...], dw.get(j)[...]) * slope.get(j)[...].astype(F32)).astype(BF)
        grad_hidden[:, cols] = grad
        sums[:, cols] = column_sum(grad)
    send[...] = half_of(grad_hidden, 1 - lax.axis_index("stream"), FH)


def where_to(plan, i):
    stream, relative = lax.axis_index("stream"), lax.axis_index("batch") ^ i
    slots = []
    for bits in plan:
        last = len(bits) - 1
        slots.append(sum((((relative >> bit) & 1) << (last - step)) for step, bit in enumerate(bits)))
    return jnp.where(stream == 0, slots[0], slots[1])


def put_chunk(part, slot, keep, send, lanes):
    here = keep.shape[0]

    @pl.when(slot < here)
    def _():
        keep[slot, :, lanes] = part

    @pl.when(slot >= here)
    def _():
        send[slot - here, :, lanes] = part


def place_rows(total, first, rows, groups, outs, start):
    if groups is None:
        outs[0][first : first + total.shape[0], start : start + total.shape[1]] = total
        return
    low = total.astype(BF)
    for n, (plan, top, height, left, width) in enumerate(groups):
        begin, end = max(left, start), min(left + width, start + total.shape[1])
        if begin >= end:
            continue
        for i in range(total.shape[0] // rows):
            piece = low[i * rows + top : i * rows + top + height, begin - start : end - start]
            put_chunk(piece, where_to(plan, first // rows + i), outs[2 * n], outs[2 * n + 1], slice(begin - left, end - left))


def outer_body(rows, groups, counts, left, left_other, *refs):
    rights, outs = refs[: 2 * len(counts)], refs[2 * len(counts) :]
    start = piece = 0
    for i, count in enumerate(counts):
        right, right_other = rights[2 * i : 2 * i + 2]
        columns = right_other.shape[1]
        mine = right[...] if right.shape[1] == columns else half_of(right, lax.axis_index("stream"), columns)
        other = right_other[...]
        for j in range(count):
            total = dot_tn(left.get(piece)[...], mine) + dot_tn(left_other.get(piece)[...], other)
            piece += 1
            place_rows(total, j * D, rows, groups, outs, start)
        start += columns


def first_body(uw, normed, scale, grad_hidden, branch, gain, attn, sums):
    grad_first = branch[...].astype(F32)
    for j in range(len(uw.refs)):
        grad_first += dot_nt(grad_hidden[:, j * D : (j + 1) * D], uw.get(j)[...])
    n = normed.get()[...].astype(F32)
    resid = norm_back(grad_first, lane(gain), n, scale.get()[...])
    attn[...] = resid.astype(BF)
    sums[0:1] = column_sum(grad_first * n)
    sums[1:2] = column_sum(grad_first)
    sums[2:3] = column_sum(attn[...])


def half_index(which):
    stream = lax.axis_index("stream")
    return stream if which else 1 - stream


def head_lanes(which):
    return lambda: (slice(None), pl.ds(pl.multiple_of(half_index(which) * HALF, 128), HALF))


def head_rows(which):
    return lambda: pl.ds(pl.multiple_of(half_index(which) * HALF, 128), HALF)


def head_pair(which, i):
    return lambda: pl.ds(half_index(which) * (HEADS // 2) + 2 * i, 2)


def attend_back_body(which, ow, v, k, q, p, attn, grads_qk, grads_v, sums):
    grad_mixed = dot_nt(attn[...], ow.get()[...]).astype(BF)
    first_lanes = lax.broadcasted_iota(jnp.int32, (LEN, 2 * HD), 1) < HD
    for i in range(PAIRS // 2):
        lanes = slice(i * 2 * HD, (i + 1) * 2 * HD)
        g2, v2, k2, q2 = grad_mixed[:, lanes], v.get()[:, lanes], k.get()[:, lanes], q.get()[:, lanes]
        zero = jnp.zeros_like(q2)
        turned = k2.T
        tq, tk, tv = [], None, None
        for half in range(2):
            keep = first_lanes if half == 0 else jnp.logical_not(first_lanes)
            probs = p.get(i)[half]
            g = jnp.where(keep, g2, zero)
            weighted = dot_nt(v2, g) * probs.astype(F32)
            inner = jnp.sum(weighted, axis=0, keepdims=True)
            raw = (weighted - probs.astype(F32) * inner).astype(BF)
            tq.append(dot(turned[half * HD : (half + 1) * HD], raw))
            parts = (dot(raw, jnp.where(keep, q2, zero)), dot(probs, g))
            tk, tv = parts if half == 0 else (tk + parts[0], tv + parts[1])
        for j, grad in enumerate((jnp.concatenate(tq, axis=0).T * 0.125, tk * 0.125, tv)):
            ref, start = (grads_v, i * 2 * HD) if j == 2 else (grads_qk, j * HALF + i * 2 * HD)
            ref[:, start : start + 2 * HD] = grad.astype(BF)
    grads_v[:, HALF:] = half_of(attn, half_index(which), HALF)
    sums[0:1] = column_sum(grads_qk[:, :HALF])
    sums[1:2] = column_sum(grads_v[:, :HALF])


VEC = ("gain2", "bias2", "down", "gain1", "bias1", "out", "query", "value")


def whole_rows(stream, away, own):
    return jnp.where(stream == 0, jnp.concatenate([own, away], axis=1), jnp.concatenate([away, own], axis=1))


def vectors_body(rows, sums2, sums1, sums_away, sums_own, sums_up, out):
    blank = jnp.zeros((128 - len(VEC), D), F32)
    sums0 = whole_rows(lax.axis_index("stream"), sums_away[0:2], sums_own[0:2])
    turned = jnp.concatenate([sums2[0:3], sums1[0:3], sums0, blank], axis=0).T
    tall = jnp.broadcast_to(sums_up[...], (128, FF)).T.reshape(D // rows, FF // D, rows, 128)
    slot = lax.broadcasted_iota(jnp.int32, (rows, 128), 1)
    for i in range(D // rows):
        piece = turned[i * rows : (i + 1) * rows]
        for part in range(FF // D):
            piece = jnp.where(slot == len(VEC) + part, tall[i, part], piece)
        out[i * rows : (i + 1) * rows] = piece.astype(BF)


def qkv_outer_body(rows, groups, left, left_other, own_qk, own_v, other_qk, other_v, *outs):
    if groups is not None:
        vectors, *outs = outs
        plan, _, _, first_lane, _ = groups[-1]
        for i in range(D // rows):
            lanes = slice(4 * HALF - first_lane, 4 * HALF - first_lane + 128)
            put_chunk(vectors[i * rows : (i + 1) * rows], where_to(plan, i), outs[-2], outs[-1], lanes)
    start = 0
    for i, (own, other) in enumerate(((own_qk, other_qk), (own_v, other_v))):
        for j in range(2):
            lanes, piece = slice(j * HALF, (j + 1) * HALF), i * j
            total = dot_tn(left.get(piece)[...], own[:, lanes]) + dot_tn(left_other.get(piece)[...], other[:, lanes])
            place_rows(total, 0, rows, groups, outs, start)
            start += HALF


def input_body(qw, kw, vw, attn, *refs):
    out = refs[-1]
    total = attn[...].astype(F32)
    for i, weight in enumerate((qw, kw, vw)):
        for which in range(2):
            grads = refs[2 * which + i // 2][:, i % 2 * HALF : (i % 2 + 1) * HALF]
            total += dot_nt(grads, weight.get(which)[...])
    out[...] = total


def add_body(keep, arrived, *outs):
    if len(outs) == 1:
        outs[0][...] = (wide(keep) + wide(arrived)).astype(BF)
        return
    half = outs[0].shape[0]
    outs[0][...] = (keep[:half].astype(F32) + arrived[:half].astype(F32)).astype(BF)
    outs[1][...] = (keep[half:].astype(F32) + arrived[half:].astype(F32)).astype(BF)


def final_body(count, pieces, vectors, *refs):
    mine, other, outs = refs[:count], refs[count : 2 * count], refs[2 * count :]
    swap = lax.axis_index("stream") != 0
    for ref, parts in zip(outs, pieces):
        middle = ref.shape[1] // 2
        at = {}
        for which, lane_from, lanes, top in parts:
            a, b = mine[which][:, lane_from : lane_from + lanes], other[which][:, lane_from : lane_from + lanes]
            rows, begin = slice(top, top + a.shape[0]), at.get(top, 0)
            ref[rows, begin : begin + lanes] = jnp.where(swap, b, a).astype(F32)
            ref[rows, middle + begin : middle + begin + lanes] = jnp.where(swap, a, b).astype(F32)
            at[top] = begin + lanes
    if vectors is not None:
        both = (mine[-1][:, vectors:].astype(F32) + other[-1][:, vectors:].astype(F32)).T
        for i, ref in enumerate(outs[len(pieces) :]):
            if i < len(VEC):
                ref[...] = both[i]
            else:
                ref[...] = jnp.concatenate([both[i + j : i + j + 1] for j in range(FF // D)], axis=1).reshape(-1)


def swap_cores(x):
    return lax.ppermute(x, "stream", [(0, 1), (1, 0)])


AXIS_BITS = {"x": 0, "y": 1, "z": 2, "w": 3}


def bit_plan(plan, batches):
    count = batches.bit_length() - 1
    return [[AXIS_BITS[axis] for axis in order] if count == len(order) else list(range(count)) for order in plan]


def halve_send(send, plan, batches, step):
    pairs = [
        (core * batches + b, core * batches + (b ^ (1 << plan[core][step]))) for core in range(2) for b in range(batches)
    ]
    return lax.ppermute(send, AXES, pairs)


def local(
    batches,
    tokens,
    seg_ids,
    pos_ids,
    q_weight,
    q_bias,
    k_weight,
    v_weight,
    v_bias,
    o_weight,
    o_bias,
    norm1_gain,
    norm1_bias,
    up_weight,
    up_bias,
    down_weight,
    down_bias,
    norm2_gain,
    norm2_bias,
):
    texts = pos_ids.shape[0]
    rows = D // batches
    chunked = rows % 16 == 0 and batches & (batches - 1) == 0
    stages = batches.bit_length() - 1
    tok, seg, pos = tokens.reshape(LEN, D), seg_ids.reshape(1, LEN), pos_ids.reshape(1, texts)
    low, sums = shape_of((LEN, D), BF), shape_of((ROWS8, D), F32)
    low_half = shape_of((LEN, HALF), BF)
    wide_low = shape_of((LEN, FF), BF)
    tall = FF // batches
    cuts = {
        "a": ("down", 0, tall // 2, 0, HALF),
        "b": ("down", tall // 2, tall // 2, 0, HALF),
        "u": ("up", 0, rows, 0, FH),
        "q": ("qkv", 0, rows, 0, 2 * HALF),
        "r": ("qkv", 0, rows, 2 * HALF, 2 * HALF + 128),
    }
    plans = {name: bit_plan(plan, batches) for name, plan in PLANS.items()}
    token = []

    def run(body, outs, args, name, micros, limit=8, **more):
        results = call(body, outs, args + after(*token), name, micros, limit if chunked else 48, **more)
        token[:] = [results[0]]
        return results

    embeds, scale1, hidden_out, act, stack, q, k, v, p, slope, normed1, tail = forward(
        2 * batches,
        tok,
        seg,
        (q_weight, k_weight, v_weight, o_weight, up_weight, down_weight),
        (q_bias, v_bias, o_bias, norm1_gain, norm1_bias, up_bias, down_bias, norm2_gain, norm2_bias),
    )
    gathered = lax.all_to_all(embeds, AXES, split_axis=0, concat_axis=0)
    act_other = swap_cores(act)
    stack_other = swap_cores(stack)
    loss, branch, branch_send, sums2 = run(
        functools.partial(loss_body, texts),
        [shape_of((1, 1), F32), low, low_half, sums],
        [near(tail), near(gathered), near(pos), near(seg), near(norm2_gain)],
        "loss",
        COSTS["loss"],
        scratch=[pltpu.VMEM((2 * batches, ROWS8, D), F32)],
    )
    branch_other = swap_cores(branch_send)
    grad_hidden, hidden_send, sums_up = run(
        hidden_body,
        [wide_low, shape_of((LEN, FH), BF), shape_of((1, FF), F32)],
        [
            late(down_weight, *[(slice(j, j + D), slice(None)) for j in range(0, FF, D)]),
            late(slope, *[lanes_of(j, D) for j in range(0, FF, D)]),
            near(branch),
        ],
        "hidden",
        COSTS["hidden"],
    )
    hidden_other = swap_cores(hidden_send)
    held, arriving, step_of, kept = {}, {}, {}, {}

    def send(name):
        if step_of[name] < stages:
            arriving[name] = halve_send(held[name][-1], plans[name], batches, step_of[name])
        else:
            arriving[name] = swap_cores(held[name][0][0])

    def add(name):
        keep, arrived = held[name][0], arriving[name]
        count = keep.shape[0]
        sizes = [count // 2] * 2 if count > 1 else [1]
        outs = [shape_of((size,) + keep.shape[1:], BF) for size in sizes]
        step_of[name] += 1
        held[name] = run(add_body, outs, [near(keep), near(arrived)], f"{name}_add{step_of[name]}", COSTS["add"])
        send(name)

    def outer(product, body, size, columns, own, other, starts, rights, others=()):
        windows = [lanes_of(start, D) for start in starts]
        args = [late(own, *windows), late(other, *windows)] + [near(x) for x in rights] + [near(x) for x in others]
        height = size // batches
        if not chunked:
            outs = [shape_of((size, columns), F32)]
            kept[product] = run(functools.partial(body, height, None), outs, args, f"outer_{product}", COSTS[product], 12)[0]
            return
        names = [name for name, cut in cuts.items() if cut[0] == product]
        groups = [(plans[name],) + cuts[name][1:] for name in names]
        outs = [shape_of((batches // 2, cuts[name][2], cuts[name][4]), BF) for name in names for _ in range(2)]
        results = run(functools.partial(body, height, groups), outs, args, f"outer_{product}", COSTS[product], 12)
        for i, name in enumerate(names):
            held[name], step_of[name] = results[2 * i : 2 * i + 2], 0
            send(name)

    def plain(*counts):
        return lambda height, groups, *refs: outer_body(height, groups, counts, *refs)

    def down():
        outer("down", plain(FF // D), FF, HALF, act, act_other, range(0, FF, D), [branch, branch_other])

    def first():
        kept["attn"], kept["sums1"] = run(
            first_body,
            [low, sums],
            [
                late(up_weight, *[lanes_of(j, D) for j in range(0, FF, D)]),
                late(normed1),
                late(scale1),
                near(grad_hidden),
                near(branch),
                near(norm1_gain),
            ],
            "first",
            COSTS["first"],
        )

    def up():
        outer("up", plain(1), D, FH, stack, stack_other, (FIRST,), [grad_hidden, hidden_other])

    def heads(which):
        lanes = head_lanes(which)
        *kept["grads", which], kept["sums", which] = run(
            functools.partial(attend_back_body, which),
            [low, low, shape_of((ROWS8, HALF), F32)],
            [
                late(o_weight, head_rows(which)),
                late(v, lanes),
                late(k, lanes),
                late(q, lanes),
                late(p, *[head_pair(which, i) for i in range(PAIRS // 2)]),
                near(kept["attn"]),
            ],
            f"attend_back{which}",
            COSTS[f"heads{which}"],
            10,
        )
        if which == 0:
            kept["grads_other"] = [swap_cores(x) for x in kept["grads", 0]]

    def qkv():
        vectors = [kept["vectors"]] if chunked else []
        columns = 4 * HALF + (128 if chunked else 0)
        rights = kept["grads", 1] + kept["grads_other"]
        outer("qkv", qkv_outer_body, D, columns, stack, stack_other, (TOKENS, MIXED), rights, vectors)

    def vectors():
        if chunked:
            each = [near(x) for x in (sums2, kept["sums1"], kept["sums", 0], kept["sums", 1], sums_up)]
            body = functools.partial(vectors_body, rows)
            kept["vectors"] = run(body, [shape_of((D, 128), BF)], each, "vectors", COSTS["add"])[0]

    def grad_tokens():
        weights = [late(w, head_lanes(0), head_lanes(1)) for w in (q_weight, k_weight, v_weight)]
        grads = [near(x) for x in [kept["attn"]] + kept["grads", 0] + kept["grads", 1]]
        kept["input"] = run(input_body, [shape_of((LEN, D), F32)], weights + grads, "input", COSTS["input"])[0]

    def finish(product, names, pieces, vectors=None):
        if chunked:
            mine, other = [held[name][0][0] for name in names], [arriving[name] for name in names]
        else:
            share = lax.psum_scatter(kept[product], "batch", scatter_dimension=0, tiled=True).astype(BF)
            mine, other = [share], [swap_cores(share)]
        height = (FF if product == "down" else D) // batches
        outs = [shape_of((height, 2 * sum(x[2] for x in parts if x[3] == 0)), F32) for parts in pieces]
        if vectors is not None:
            outs += [shape_of((rows,), F32)] * len(VEC) + [shape_of((tall,), F32)]
        args = [near(x) for x in mine + other]
        return run(functools.partial(final_body, len(mine), pieces, vectors), outs, args, f"final_{names[-1]}", COSTS["end"])

    def finish_down():
        pieces = [(0, 0, HALF, 0), (1, 0, HALF, tall // 2)] if chunked else [(0, 0, HALF, 0)]
        kept["g_down"] = finish("down", "ab", [pieces])[0]

    def finish_up():
        kept["g_up"] = finish("up", "u", [[(0, 0, FH, 0)]])[0]

    def finish_qkv():
        where = ((0, 0), (0, HALF), (1, 0), (1, HALF)) if chunked else [(0, i * HALF) for i in range(4)]
        pieces = [[(which, start, HALF, 0)] for which, start in where]
        results = finish("qkv", "qr", pieces, 2 * HALF if chunked else None)
        kept["g_q"], kept["g_k"], kept["g_v"], kept["g_o"], *kept["vec"] = results

    work = {
        "down": down,
        "first": first,
        "up": up,
        "heads0": lambda: heads(0),
        "heads1": lambda: heads(1),
        "vectors": vectors,
        "qkv": qkv,
        "input": grad_tokens,
        "end_down": finish_down,
        "end_up": finish_up,
        "end_qkv": finish_qkv,
    }
    for item in ORDER:
        if item in work:
            work[item]()
        elif chunked:
            add(item)
    if chunked:
        gain2, bias2, down_b, gain1, bias1, out_b, query_b, value_b, up_b = kept["vec"]
    else:
        sums1, sums0 = kept["sums1"], whole_rows(lax.axis_index("stream"), kept["sums", 0], kept["sums", 1])
        each = [sums2[0], sums2[1], sums2[2], sums1[0], sums1[1], sums1[2], sums0[0], sums0[1], sums_up[0]]
        each = [lax.psum(lax.psum_scatter(x, "batch", scatter_dimension=0, tiled=True), "stream") for x in each]
        gain2, bias2, down_b, gain1, bias1, out_b, query_b, value_b, up_b = each
    return (
        loss.reshape(()),
        hidden_out.reshape(tokens.shape),
        kept["input"].reshape(tokens.shape),
        kept["g_q"],
        query_b,
        kept["g_k"],
        kept["g_v"],
        value_b,
        kept["g_o"],
        out_b,
        gain1,
        bias1,
        kept["g_up"],
        up_b,
        kept["g_down"],
        down_b,
        gain2,
        bias2,
    )


def solution(mesh):
    batches = mesh.shape["batch"]
    held = P("stream", "batch", None)
    split, rows = P("batch"), P("batch", None)
    return jax.shard_map(
        functools.partial(local, batches),
        mesh=mesh,
        in_specs=(held, held) + (P(),) * 16,
        out_specs=(P(), held, held, rows, split, rows, rows, split, rows, split, split, split, rows, split, rows, split, split, split),
        check_vma=False,
    )
```

```python
import functools

import jax
import jax.numpy as jnp
import numpy as np
from jax import lax
from jax.experimental import pallas as pl
from jax.experimental.pallas import tpu as pltpu
from jax.sharding import PartitionSpec as P

D = 768
HEADS = 12
HD = 64
LEN = 512
SEGS = 4
FF = 3072
HALF = D // 2
FH = FF // 2
PAIRS = HEADS // 2
ROWS8 = 8
MIB = 1 << 20
AXES = ("stream", "batch")
BF = jnp.bfloat16
F32 = jnp.float32
EPS = 1e-06
LOG2E = 1.4426950408889634
VECTORS = 16
COST_RATE = 1.15e9
COSTS = {"loss": 3.0, "hidden": 3.5, "down": 60.0, "first": 60.0, "up": 0.1, "heads0": 0.1, "heads1": 30.0, "qkv": 0.1, "input": 0.1, "add": 3.0, "end": 0.6}
PLANS = {
    "a": ("xwyz", "zxyw"),
    "b": ("ywxz", "yzxw"),
    "u": ("xwyz", "zyxw"),
    "q": ("xyzw", "zxyw"),
    "r": ("xzyw", "yxwz"),
}
ORDER = ("down", "first", "up", "heads0", *"ab", "heads1", "vectors", "qkv", "input", *"uabqruabqruabq", *"ru", "end_down", "q", "r", "end_up", "end_qkv")


def shape_of(shape, dtype):
    return jax.ShapeDtypeStruct(tuple(shape), dtype)


def cost(micros):
    return pl.CostEstimate(flops=int(micros * COST_RATE) + 1, bytes_accessed=0, transcendentals=0)


class Pieces:
    def __init__(self, ref, places):
        self.refs, self.places = [ref] * len(places), places

    def get(self, i=0):
        return window(self.refs[i], self.places[i])


def near(x):
    return ("near", x)


def after(*arrays):
    return [("after", x) for x in arrays]


def late(x, *places):
    return ("late", x, places or ((),))


def window(ref, index):
    return ref.at[index] if index != () else ref


def call(body, outs, args, name, micros, limit=8, scratch=()):
    spaces = {"near": pltpu.VMEM, "after": pl.ANY, "late": pltpu.VMEM}

    def whole(*refs):
        ins, rest = refs[: len(args)], refs[len(args) :]
        operands = []
        for arg, ref in zip(args, ins):
            if arg[0] == "late":
                operands.append(Pieces(ref, [x() if callable(x) else x for x in arg[2]]))
            elif arg[0] != "after":
                operands.append(ref)
        body(*operands, *rest)

    return pl.pallas_call(
        whole,
        out_shape=outs,
        in_specs=[pl.BlockSpec(memory_space=spaces[arg[0]]) for arg in args],
        out_specs=[pl.BlockSpec(memory_space=pltpu.VMEM)] * len(outs),
        scratch_shapes=list(scratch),
        compiler_params=pltpu.CompilerParams(vmem_limit_bytes=limit * MIB),
        cost_estimate=cost(micros),
        name=name,
    )(*[arg[1] for arg in args])


def lanes_of(start, width):
    return (slice(None), slice(start, start + width))


def dot(left, right):
    return jnp.dot(left, right, preferred_element_type=F32)


def dot_nt(left, right):
    return lax.dot_general(left, right, (((1,), (1,)), ((), ())), preferred_element_type=F32)


def dot_tn(left, right):
    return lax.dot_general(left, right, (((0,), (0,)), ((), ())), preferred_element_type=F32)


def wide(ref):
    return ref[...].astype(F32)


FIRST, MIXED, TOKENS, STACK = 0, D, 2 * D, 3 * D


def normalize(x):
    center = jnp.mean(x, axis=-1, keepdims=True)
    offset = x - center
    spread = jnp.mean(offset * offset, axis=-1, keepdims=True)
    scale = lax.rsqrt(spread + EPS)
    return offset * scale, scale


def thirds(x):
    high = x.astype(BF).astype(F32)
    middle = (x - high).astype(BF).astype(F32)
    return high, middle, x - high - middle


def lane(ref):
    return ref[...].astype(F32).reshape(1, -1)


def segment_counts(seg_row, seg):
    return jnp.sum((seg_row == seg).astype(F32), axis=-1, keepdims=True)


def column_of(seg_row):
    return jnp.broadcast_to(seg_row.astype(F32), (128, LEN)).T[:, :1].astype(jnp.int32)


def forward_body(
    tok_h, seg, qw_h, kw_h, vw_h, ow_h, uw_h, dw_h, qb, vb, ob, gain1, shift1, ub, db, gain2, shift2,
    embeds, scale1, out_h, act_h, stack_h, q_h, k_h, v_h, p_h, slope_h, normed1_h, tail_h,
    qw, kw, vw, ow, uw, dw, out, act, stack, q, k, v, p, slope, normed1, tail, bias, kept, sems,
):
    tokens = stack.at[:, TOKENS:STACK]
    loads = [
        pltpu.make_async_copy(src, dst, sems.at[i])
        for i, (src, dst) in enumerate(
            ((tok_h, tokens), (qw_h, qw), (kw_h, kw), (vw_h, vw), (ow_h, ow), (uw_h, uw), (dw_h, dw))
        )
    ]
    for load in loads[:4]:
        load.start()
    stores = []

    def store(source, home):
        copy = pltpu.make_async_copy(source, home, sems.at[len(loads) + len(stores)])
        copy.start()
        stores.append(copy)

    owner = column_of(seg[...])
    bias[...] = jnp.where(owner == seg[...], 0.0, -1e30)
    loads[0].wait()
    x = stack[:, TOKENS:STACK]
    for weight, load, shift, ref, home in (
        (qw, loads[1], qb, q, q_h), (kw, loads[2], None, k, k_h), (vw, loads[3], vb, v, v_h)
    ):
        load.wait()
        y = dot(x, weight[...])
        ref[...] = (y if shift is None else y + lane(shift)).astype(BF)
        store(ref, home)

    for load in loads[4:]:
        load.start()
    first_rows = lax.broadcasted_iota(jnp.int32, (LEN, 2 * HD), 1) < HD

    def pair(i, carry):
        lanes = pl.ds(pl.multiple_of(i * 2 * HD, 2 * HD), 2 * HD)
        q2, k2 = q[:, lanes], k[:, lanes]
        turned = v[:, lanes].T
        zero = jnp.zeros_like(q2)
        parts = []
        for half in range(2):
            keep = first_rows if half == 0 else jnp.logical_not(first_rows)
            scores = dot_nt(jnp.where(keep, k2, zero), q2) + bias[...]
            peak = jnp.max(scores, axis=0, keepdims=True)
            expo = jnp.exp2((scores - peak) * (0.125 * LOG2E))
            total = jnp.sum(expo, axis=0, keepdims=True)
            probs = (expo * (1.0 / total)).astype(BF)
            p[2 * i + half] = probs
            parts.append(dot(turned[half * HD : (half + 1) * HD], probs))
        mixed = jnp.concatenate(parts, axis=0).T.astype(BF)
        stack[:, pl.ds(pl.multiple_of(MIXED + i * 2 * HD, 2 * HD), 2 * HD)] = mixed
        return carry

    for i in range(PAIRS):
        pair(i, 0)
    store(p, p_h)
    loads[4].wait()
    x = stack[:, TOKENS:STACK].astype(F32) + dot(stack[:, MIXED:TOKENS], ow[...]) + lane(ob)
    n, s = normalize(x)
    normed1[...] = n.astype(BF)
    store(normed1, normed1_h)
    scale1[...] = s
    kept[...] = n * lane(gain1) + lane(shift1)
    stack[:, FIRST:MIXED] = kept[...].astype(BF)
    store(stack, stack_h)
    loads[5].wait()
    loads[6].wait()
    low = stack[:, FIRST:MIXED]
    total = None
    for start in range(0, FF, D):
        cols = slice(start, start + D)
        hidden = dot(low, uw[:, cols]) + ub[cols].astype(F32).reshape(1, -1)
        phi = 0.5 * (1.0 + lax.erf(hidden * 0.7071067811865476))
        low_act = (hidden * phi).astype(BF)
        act[:, cols] = low_act
        density = jnp.exp2(hidden * hidden * (-0.5 * LOG2E)) * 0.3989422804014327
        slope[:, cols] = (phi + hidden * density).astype(BF)
        store(act.at[:, cols], act_h.at[:, cols])
        store(slope.at[:, cols], slope_h.at[:, cols])
        part = dot(low_act, dw[cols, :])
        total = part if total is None else total + part
    n, s = normalize(kept[...] + total + lane(db))
    tail[:LEN, :D] = n.astype(BF)
    slot = lax.broadcasted_iota(jnp.int32, (LEN, 128), 1)
    high, middle, low_part = thirds(s)
    tail[:LEN, D:] = jnp.where(slot == 0, high, jnp.where(slot == 1, middle, jnp.where(slot == 2, low_part, 0.0))).astype(BF)
    store(tail.at[:LEN], tail_h.at[:LEN])
    second = n * lane(gain2) + lane(shift2)
    out[...] = second.astype(BF)
    store(out, out_h)
    rows = lax.broadcasted_iota(jnp.int32, (ROWS8, D), 0)
    pooled = jnp.zeros((ROWS8, D), F32)
    for text in range(SEGS):
        mean = jnp.sum(jnp.where(owner == text, second, 0.0), axis=0, keepdims=True) / segment_counts(seg[...], text)
        pooled = jnp.where(rows == text, mean, pooled)
    for i, part in enumerate(thirds(pooled)):
        rows16 = slice(LEN + 16 * i, LEN + 16 * i + 16)
        tail[rows16, :D] = jnp.concatenate([part, jnp.zeros_like(part)], axis=0).astype(BF)
        tail[rows16, D:] = jnp.zeros((16, 128), BF)
    store(tail.at[LEN:], tail_h.at[LEN:])
    embed = (pooled * lax.rsqrt(jnp.sum(pooled * pooled, axis=-1, keepdims=True) + EPS)).astype(BF)[:SEGS]
    for i in range(embeds.shape[0]):
        embeds[i] = embed
    for copy in stores:
        copy.wait()


def forward(devices, tok, seg, weights, vectors):
    here, away = pl.BlockSpec(memory_space=pltpu.VMEM), pl.BlockSpec(memory_space=pltpu.HBM)
    low, full, square = ((LEN, D), BF), ((LEN, D), F32), ((D, D), BF)
    outs = [((devices, SEGS, D), BF), ((LEN, 1), F32)]
    saved = [low, ((LEN, FF), BF), ((LEN, STACK), BF), low, low, low, ((HEADS, LEN, LEN), BF), ((LEN, FF), BF), low, ((LEN + 48, D + 128), BF)]
    scratch = [square] * 4 + [((D, FF), BF), ((FF, D), BF)] + saved + [((LEN, LEN), F32), full]
    return pl.pallas_call(
        forward_body,
        out_shape=[shape_of(*x) for x in outs + saved],
        in_specs=[away, here] + [away] * 6 + [here] * 9,
        out_specs=[here] * len(outs) + [away] * len(saved),
        scratch_shapes=[pltpu.VMEM(*x) for x in scratch] + [pltpu.SemaphoreType.DMA((7 + len(saved) + 7,))],
        compiler_params=pltpu.CompilerParams(vmem_limit_bytes=56 * MIB),
        cost_estimate=cost(25.0),
        name="forward",
    )(tok, seg, *weights, *vectors)


def half_of(ref, index, width):
    return ref[:, pl.ds(pl.multiple_of(index * width, 128), width)]


def norm_back(grad_out, gain, normed, scale):
    weighted = grad_out * gain
    mean_plain = jnp.mean(weighted, axis=-1, keepdims=True)
    mean_cross = jnp.mean(weighted * normed, axis=-1, keepdims=True)
    return scale * (weighted - mean_plain - normed * mean_cross)


def column_sum(x):
    return jnp.sum(x.astype(F32), axis=0, keepdims=True)


def loss_body(texts, tail, gathered, pos, seg, gain, loss, branch, branch_send, sums, tall):
    stream, batch = lax.axis_index("stream"), lax.axis_index("batch")
    for i in range(gathered.shape[0]):
        tall[i, :SEGS] = gathered[i].astype(F32)
        tall[i, SEGS:] = jnp.zeros((ROWS8 - SEGS, D), F32)
    every = tall[...].reshape(4 * texts, D).astype(BF)
    span = 2 * texts
    row = lax.broadcasted_iota(jnp.int32, (texts, span), 0)
    col = lax.broadcasted_iota(jnp.int32, (texts, span), 1)
    pick = (col == (row // SEGS) * ROWS8 + row % SEGS).astype(F32).astype(BF)
    query = dot(pick, every[:span]).astype(BF)
    passage = dot(pick, every[span:]).astype(BF)
    scores = dot_nt(passage, query) * 100.0
    peak = jnp.max(scores, axis=0, keepdims=True)
    log_total = peak + jnp.log(jnp.sum(jnp.exp(scores - peak), axis=0, keepdims=True))
    chosen = (lax.broadcasted_iota(jnp.int32, (texts, texts), 0) == pos[...]).astype(F32)
    losses = log_total - jnp.sum(chosen * scores, axis=0, keepdims=True)
    loss[...] = jnp.sum(losses, axis=1, keepdims=True) / texts
    grad_scores = ((jnp.exp(scores - log_total) - chosen) / texts).astype(BF)
    row = lax.broadcasted_iota(jnp.int32, (ROWS8, texts), 0)
    col = lax.broadcasted_iota(jnp.int32, (ROWS8, texts), 1)
    mine = jnp.logical_and(col == batch * SEGS + row, row < SEGS).astype(F32).astype(BF)
    to_query = dot(dot_nt(mine, grad_scores).astype(BF), passage)
    to_passage = dot(dot(mine, grad_scores).astype(BF), query)
    grad_embed = jnp.where(stream == 0, to_query, to_passage) * 100.0
    pooled = sum(tail[LEN + 16 * i : LEN + 16 * i + 16, :D].astype(F32) for i in range(3))[:ROWS8]
    inverse = lax.rsqrt(jnp.sum(pooled * pooled, axis=-1, keepdims=True) + EPS)
    cross = jnp.sum(grad_embed * pooled, axis=-1, keepdims=True)
    grad_pooled = inverse * grad_embed - pooled * (inverse * inverse * inverse * cross)
    owner = column_of(seg[...])
    grad_second = jnp.zeros((LEN, D), F32)
    for text in range(SEGS):
        share = grad_pooled[text : text + 1] / segment_counts(seg[...], text)
        grad_second = jnp.where(owner == text, share, grad_second)
    n = tail[:LEN, :D].astype(F32)
    scale = sum(tail[:LEN, D:].astype(F32)[:, i : i + 1] for i in range(3))
    resid = norm_back(grad_second, lane(gain), n, scale)
    branch[...] = resid.astype(BF)
    branch_send[...] = half_of(branch, 1 - stream, HALF)
    sums[0:1] = column_sum(grad_second * n)
    sums[1:2] = column_sum(grad_second)
    sums[2:3] = column_sum(branch[...])


def hidden_body(dw, slope, branch, grad_hidden, send, sums):
    for j in range(len(dw.refs)):
        cols = slice(j * D, (j + 1) * D)
        grad = (dot_nt(branch[...], dw.get(j)[...]) * slope.get(j)[...].astype(F32)).astype(BF)
        grad_hidden[:, cols] = grad
        sums[:, cols] = column_sum(grad)
    send[...] = half_of(grad_hidden, 1 - lax.axis_index("stream"), FH)


def where_to(plan, i):
    stream, relative = lax.axis_index("stream"), lax.axis_index("batch") ^ i
    slots = []
    for bits in plan:
        last = len(bits) - 1
        slots.append(sum((((relative >> bit) & 1) << (last - step)) for step, bit in enumerate(bits)))
    return jnp.where(stream == 0, slots[0], slots[1])


def put_chunk(part, slot, keep, send, lanes):
    here = keep.shape[0]

    @pl.when(slot < here)
    def _():
        keep[slot, :, lanes] = part

    @pl.when(slot >= here)
    def _():
        send[slot - here, :, lanes] = part


def place_rows(total, first, rows, groups, outs, start):
    if groups is None:
        outs[0][first : first + total.shape[0], start : start + total.shape[1]] = total
        return
    low = total.astype(BF)
    for n, (plan, top, height, left, width) in enumerate(groups):
        begin, end = max(left, start), min(left + width, start + total.shape[1])
        if begin >= end:
            continue
        for i in range(total.shape[0] // rows):
            piece = low[i * rows + top : i * rows + top + height, begin - start : end - start]
            put_chunk(piece, where_to(plan, first // rows + i), outs[2 * n], outs[2 * n + 1], slice(begin - left, end - left))


def outer_body(rows, groups, counts, left, left_other, *refs):
    rights, outs = refs[: 2 * len(counts)], refs[2 * len(counts) :]
    start = piece = 0
    for i, count in enumerate(counts):
        right, right_other = rights[2 * i : 2 * i + 2]
        columns = right_other.shape[1]
        mine = right[...] if right.shape[1] == columns else half_of(right, lax.axis_index("stream"), columns)
        other = right_other[...]
        for j in range(count):
            total = dot_tn(left.get(piece)[...], mine) + dot_tn(left_other.get(piece)[...], other)
            piece += 1
            place_rows(total, j * D, rows, groups, outs, start)
        start += columns


def first_body(uw, normed, scale, grad_hidden, branch, gain, attn, sums):
    grad_first = branch[...].astype(F32)
    for j in range(len(uw.refs)):
        grad_first += dot_nt(grad_hidden[:, j * D : (j + 1) * D], uw.get(j)[...])
    n = normed.get()[...].astype(F32)
    resid = norm_back(grad_first, lane(gain), n, scale.get()[...])
    attn[...] = resid.astype(BF)
    sums[0:1] = column_sum(grad_first * n)
    sums[1:2] = column_sum(grad_first)
    sums[2:3] = column_sum(attn[...])


def half_index(which):
    stream = lax.axis_index("stream")
    return stream if which else 1 - stream


def head_lanes(which):
    return lambda: (slice(None), pl.ds(pl.multiple_of(half_index(which) * HALF, 128), HALF))


def head_rows(which):
    return lambda: pl.ds(pl.multiple_of(half_index(which) * HALF, 128), HALF)


def head_pair(which, i):
    return lambda: pl.ds(half_index(which) * (HEADS // 2) + 2 * i, 2)


def attend_back_body(which, ow, v, k, q, p, attn, grads_qk, grads_v, sums):
    grad_mixed = dot_nt(attn[...], ow.get()[...]).astype(BF)
    first_lanes = lax.broadcasted_iota(jnp.int32, (LEN, 2 * HD), 1) < HD
    for i in range(PAIRS // 2):
        lanes = slice(i * 2 * HD, (i + 1) * 2 * HD)
        g2, v2, k2, q2 = grad_mixed[:, lanes], v.get()[:, lanes], k.get()[:, lanes], q.get()[:, lanes]
        zero = jnp.zeros_like(q2)
        turned = k2.T
        tq, tk, tv = [], None, None
        for half in range(2):
            keep = first_lanes if half == 0 else jnp.logical_not(first_lanes)
            probs = p.get(i)[half]
            g = jnp.where(keep, g2, zero)
            weighted = dot_nt(v2, g) * probs.astype(F32)
            inner = jnp.sum(weighted, axis=0, keepdims=True)
            raw = (weighted - probs.astype(F32) * inner).astype(BF)
            tq.append(dot(turned[half * HD : (half + 1) * HD], raw))
            parts = (dot(raw, jnp.where(keep, q2, zero)), dot(probs, g))
            tk, tv = parts if half == 0 else (tk + parts[0], tv + parts[1])
        for j, grad in enumerate((jnp.concatenate(tq, axis=0).T * 0.125, tk * 0.125, tv)):
            ref, start = (grads_v, i * 2 * HD) if j == 2 else (grads_qk, j * HALF + i * 2 * HD)
            ref[:, start : start + 2 * HD] = grad.astype(BF)
    grads_v[:, HALF:] = half_of(attn, half_index(which), HALF)
    sums[0:1] = column_sum(grads_qk[:, :HALF])
    sums[1:2] = column_sum(grads_v[:, :HALF])


VEC = ("gain2", "bias2", "down", "gain1", "bias1", "out", "query", "value")


def whole_rows(stream, away, own):
    return jnp.where(stream == 0, jnp.concatenate([own, away], axis=1), jnp.concatenate([away, own], axis=1))


def vectors_body(rows, sums2, sums1, sums_away, sums_own, sums_up, out):
    blank = jnp.zeros((128 - len(VEC), D), F32)
    sums0 = whole_rows(lax.axis_index("stream"), sums_away[0:2], sums_own[0:2])
    turned = jnp.concatenate([sums2[0:3], sums1[0:3], sums0, blank], axis=0).T
    tall = jnp.broadcast_to(sums_up[...], (128, FF)).T.reshape(D // rows, FF // D, rows, 128)
    slot = lax.broadcasted_iota(jnp.int32, (rows, 128), 1)
    for i in range(D // rows):
        piece = turned[i * rows : (i + 1) * rows]
        for part in range(FF // D):
            piece = jnp.where(slot == len(VEC) + part, tall[i, part], piece)
        out[i * rows : (i + 1) * rows] = piece.astype(BF)


def qkv_outer_body(rows, groups, left, left_other, own_qk, own_v, other_qk, other_v, *outs):
    if groups is not None:
        vectors, *outs = outs
        plan, _, _, first_lane, _ = groups[-1]
        for i in range(D // rows):
            lanes = slice(4 * HALF - first_lane, 4 * HALF - first_lane + 128)
            put_chunk(vectors[i * rows : (i + 1) * rows], where_to(plan, i), outs[-2], outs[-1], lanes)
    start = 0
    for i, (own, other) in enumerate(((own_qk, other_qk), (own_v, other_v))):
        for j in range(2):
            lanes, piece = slice(j * HALF, (j + 1) * HALF), i * j
            total = dot_tn(left.get(piece)[...], own[:, lanes]) + dot_tn(left_other.get(piece)[...], other[:, lanes])
            place_rows(total, 0, rows, groups, outs, start)
            start += HALF


def input_body(qw, kw, vw, attn, *refs):
    out = refs[-1]
    total = attn[...].astype(F32)
    for i, weight in enumerate((qw, kw, vw)):
        for which in range(2):
            grads = refs[2 * which + i // 2][:, i % 2 * HALF : (i % 2 + 1) * HALF]
            total += dot_nt(grads, weight.get(which)[...])
    out[...] = total


def add_body(keep, arrived, *outs):
    if len(outs) == 1:
        outs[0][...] = (wide(keep) + wide(arrived)).astype(BF)
        return
    half = outs[0].shape[0]
    outs[0][...] = (keep[:half].astype(F32) + arrived[:half].astype(F32)).astype(BF)
    outs[1][...] = (keep[half:].astype(F32) + arrived[half:].astype(F32)).astype(BF)


def final_body(count, pieces, vectors, *refs):
    mine, other, outs = refs[:count], refs[count : 2 * count], refs[2 * count :]
    swap = lax.axis_index("stream") != 0
    for ref, parts in zip(outs, pieces):
        middle = ref.shape[1] // 2
        at = {}
        for which, lane_from, lanes, top in parts:
            a, b = mine[which][:, lane_from : lane_from + lanes], other[which][:, lane_from : lane_from + lanes]
            rows, begin = slice(top, top + a.shape[0]), at.get(top, 0)
            ref[rows, begin : begin + lanes] = jnp.where(swap, b, a).astype(F32)
            ref[rows, middle + begin : middle + begin + lanes] = jnp.where(swap, a, b).astype(F32)
            at[top] = begin + lanes
    if vectors is not None:
        both = (mine[-1][:, vectors:].astype(F32) + other[-1][:, vectors:].astype(F32)).T
        for i, ref in enumerate(outs[len(pieces) :]):
            if i < len(VEC):
                ref[...] = both[i]
            else:
                ref[...] = jnp.concatenate([both[i + j : i + j + 1] for j in range(FF // D)], axis=1).reshape(-1)


def swap_cores(x):
    return lax.ppermute(x, "stream", [(0, 1), (1, 0)])


AXIS_BITS = {"x": 0, "y": 1, "z": 2, "w": 3}


def bit_plan(plan, batches):
    count = batches.bit_length() - 1
    return [[AXIS_BITS[axis] for axis in order] if count == len(order) else list(range(count)) for order in plan]


def halve_send(send, plan, batches, step):
    pairs = [
        (core * batches + b, core * batches + (b ^ (1 << plan[core][step]))) for core in range(2) for b in range(batches)
    ]
    return lax.ppermute(send, AXES, pairs)


def local(
    batches,
    tokens,
    seg_ids,
    pos_ids,
    q_weight,
    q_bias,
    k_weight,
    v_weight,
    v_bias,
    o_weight,
    o_bias,
    norm1_gain,
    norm1_bias,
    up_weight,
    up_bias,
    down_weight,
    down_bias,
    norm2_gain,
    norm2_bias,
):
    texts = pos_ids.shape[0]
    rows = D // batches
    chunked = rows % 16 == 0 and batches & (batches - 1) == 0
    stages = batches.bit_length() - 1
    tok, seg, pos = tokens.reshape(LEN, D), seg_ids.reshape(1, LEN), pos_ids.reshape(1, texts)
    low, sums = shape_of((LEN, D), BF), shape_of((ROWS8, D), F32)
    low_half = shape_of((LEN, HALF), BF)
    wide_low = shape_of((LEN, FF), BF)
    tall = FF // batches
    cuts = {
        "a": ("down", 0, tall // 2, 0, HALF),
        "b": ("down", tall // 2, tall // 2, 0, HALF),
        "u": ("up", 0, rows, 0, FH),
        "q": ("qkv", 0, rows, 0, 2 * HALF),
        "r": ("qkv", 0, rows, 2 * HALF, 2 * HALF + 128),
    }
    plans = {name: bit_plan(plan, batches) for name, plan in PLANS.items()}
    token = []

    def run(body, outs, args, name, micros, limit=8, **more):
        results = call(body, outs, args + after(*token), name, micros, limit if chunked else 48, **more)
        token[:] = [results[0]]
        return results

    embeds, scale1, hidden_out, act, stack, q, k, v, p, slope, normed1, tail = forward(
        2 * batches,
        tok,
        seg,
        (q_weight, k_weight, v_weight, o_weight, up_weight, down_weight),
        (q_bias, v_bias, o_bias, norm1_gain, norm1_bias, up_bias, down_bias, norm2_gain, norm2_bias),
    )
    gathered = lax.all_to_all(embeds, AXES, split_axis=0, concat_axis=0)
    act_other = swap_cores(act)
    stack_other = swap_cores(stack)
    loss, branch, branch_send, sums2 = run(
        functools.partial(loss_body, texts),
        [shape_of((1, 1), F32), low, low_half, sums],
        [near(tail), near(gathered), near(pos), near(seg), near(norm2_gain)],
        "loss",
        COSTS["loss"],
        scratch=[pltpu.VMEM((2 * batches, ROWS8, D), F32)],
    )
    branch_other = swap_cores(branch_send)
    grad_hidden, hidden_send, sums_up = run(
        hidden_body,
        [wide_low, shape_of((LEN, FH), BF), shape_of((1, FF), F32)],
        [
            late(down_weight, *[(slice(j, j + D), slice(None)) for j in range(0, FF, D)]),
            late(slope, *[lanes_of(j, D) for j in range(0, FF, D)]),
            near(branch),
        ],
        "hidden",
        COSTS["hidden"],
    )
    hidden_other = swap_cores(hidden_send)
    held, arriving, step_of, kept = {}, {}, {}, {}

    def send(name):
        if step_of[name] < stages:
            arriving[name] = halve_send(held[name][-1], plans[name], batches, step_of[name])
        else:
            arriving[name] = swap_cores(held[name][0][0])

    def add(name):
        keep, arrived = held[name][0], arriving[name]
        count = keep.shape[0]
        sizes = [count // 2] * 2 if count > 1 else [1]
        outs = [shape_of((size,) + keep.shape[1:], BF) for size in sizes]
        step_of[name] += 1
        held[name] = run(add_body, outs, [near(keep), near(arrived)], f"{name}_add{step_of[name]}", COSTS["add"])
        send(name)

    def outer(product, body, size, columns, own, other, starts, rights, others=()):
        windows = [lanes_of(start, D) for start in starts]
        args = [late(own, *windows), late(other, *windows)] + [near(x) for x in rights] + [near(x) for x in others]
        height = size // batches
        if not chunked:
            outs = [shape_of((size, columns), F32)]
            kept[product] = run(functools.partial(body, height, None), outs, args, f"outer_{product}", COSTS[product], 12)[0]
            return
        names = [name for name, cut in cuts.items() if cut[0] == product]
        groups = [(plans[name],) + cuts[name][1:] for name in names]
        outs = [shape_of((batches // 2, cuts[name][2], cuts[name][4]), BF) for name in names for _ in range(2)]
        results = run(functools.partial(body, height, groups), outs, args, f"outer_{product}", COSTS[product], 12)
        for i, name in enumerate(names):
            held[name], step_of[name] = results[2 * i : 2 * i + 2], 0
            send(name)

    def plain(*counts):
        return lambda height, groups, *refs: outer_body(height, groups, counts, *refs)

    def down():
        outer("down", plain(FF // D), FF, HALF, act, act_other, range(0, FF, D), [branch, branch_other])

    def first():
        kept["attn"], kept["sums1"] = run(
            first_body,
            [low, sums],
            [
                late(up_weight, *[lanes_of(j, D) for j in range(0, FF, D)]),
                late(normed1),
                late(scale1),
                near(grad_hidden),
                near(branch),
                near(norm1_gain),
            ],
            "first",
            COSTS["first"],
        )

    def up():
        outer("up", plain(1), D, FH, stack, stack_other, (FIRST,), [grad_hidden, hidden_other])

    def heads(which):
        lanes = head_lanes(which)
        *kept["grads", which], kept["sums", which] = run(
            functools.partial(attend_back_body, which),
            [low, low, shape_of((ROWS8, HALF), F32)],
            [
                late(o_weight, head_rows(which)),
                late(v, lanes),
                late(k, lanes),
                late(q, lanes),
                late(p, *[head_pair(which, i) for i in range(PAIRS // 2)]),
                near(kept["attn"]),
            ],
            f"attend_back{which}",
            COSTS[f"heads{which}"],
            10,
        )
        if which == 0:
            kept["grads_other"] = [swap_cores(x) for x in kept["grads", 0]]

    def qkv():
        vectors = [kept["vectors"]] if chunked else []
        columns = 4 * HALF + (128 if chunked else 0)
        rights = kept["grads", 1] + kept["grads_other"]
        outer("qkv", qkv_outer_body, D, columns, stack, stack_other, (TOKENS, MIXED), rights, vectors)

    def vectors():
        if chunked:
            each = [near(x) for x in (sums2, kept["sums1"], kept["sums", 0], kept["sums", 1], sums_up)]
            body = functools.partial(vectors_body, rows)
            kept["vectors"] = run(body, [shape_of((D, 128), BF)], each, "vectors", COSTS["add"])[0]

    def grad_tokens():
        weights = [late(w, head_lanes(0), head_lanes(1)) for w in (q_weight, k_weight, v_weight)]
        grads = [near(x) for x in [kept["attn"]] + kept["grads", 0] + kept["grads", 1]]
        kept["input"] = run(input_body, [shape_of((LEN, D), F32)], weights + grads, "input", COSTS["input"])[0]

    def finish(product, names, pieces, vectors=None):
        if chunked:
            mine, other = [held[name][0][0] for name in names], [arriving[name] for name in names]
        else:
            share = lax.psum_scatter(kept[product], "batch", scatter_dimension=0, tiled=True).astype(BF)
            mine, other = [share], [swap_cores(share)]
        height = (FF if product == "down" else D) // batches
        outs = [shape_of((height, 2 * sum(x[2] for x in parts if x[3] == 0)), F32) for parts in pieces]
        if vectors is not None:
            outs += [shape_of((rows,), F32)] * len(VEC) + [shape_of((tall,), F32)]
        args = [near(x) for x in mine + other]
        return run(functools.partial(final_body, len(mine), pieces, vectors), outs, args, f"final_{names[-1]}", COSTS["end"])

    def finish_down():
        pieces = [(0, 0, HALF, 0), (1, 0, HALF, tall // 2)] if chunked else [(0, 0, HALF, 0)]
        kept["g_down"] = finish("down", "ab", [pieces])[0]

    def finish_up():
        if not chunked:
            kept["g_up"] = finish("up", "u", [[(0, 0, FH, 0)]])[0]

    def finish_qkv():
        if chunked:
            where = ((0, 0, FH), (1, 0, HALF), (1, HALF, HALF), (2, 0, HALF), (2, HALF, HALF))
            pieces = [[(which, start, lanes, 0)] for which, start, lanes in where]
            kept["g_up"], *results = finish("qkv", "uqr", pieces, 2 * HALF)
        else:
            results = finish("qkv", "qr", [[(0, i * HALF, HALF, 0)] for i in range(4)])
        kept["g_q"], kept["g_k"], kept["g_v"], kept["g_o"], *kept["vec"] = results

    work = {
        "down": down,
        "first": first,
        "up": up,
        "heads0": lambda: heads(0),
        "heads1": lambda: heads(1),
        "vectors": vectors,
        "qkv": qkv,
        "input": grad_tokens,
        "end_down": finish_down,
        "end_up": finish_up,
        "end_qkv": finish_qkv,
    }
    for item in ORDER:
        if item in work:
            work[item]()
        elif chunked:
            add(item)
    if chunked:
        gain2, bias2, down_b, gain1, bias1, out_b, query_b, value_b, up_b = kept["vec"]
    else:
        sums1, sums0 = kept["sums1"], whole_rows(lax.axis_index("stream"), kept["sums", 0], kept["sums", 1])
        each = [sums2[0], sums2[1], sums2[2], sums1[0], sums1[1], sums1[2], sums0[0], sums0[1], sums_up[0]]
        each = [lax.psum(lax.psum_scatter(x, "batch", scatter_dimension=0, tiled=True), "stream") for x in each]
        gain2, bias2, down_b, gain1, bias1, out_b, query_b, value_b, up_b = each
    return (
        loss.reshape(()),
        hidden_out.reshape(tokens.shape),
        kept["input"].reshape(tokens.shape),
        kept["g_q"],
        query_b,
        kept["g_k"],
        kept["g_v"],
        value_b,
        kept["g_o"],
        out_b,
        gain1,
        bias1,
        kept["g_up"],
        up_b,
        kept["g_down"],
        down_b,
        gain2,
        bias2,
    )


def solution(mesh):
    batches = mesh.shape["batch"]
    held = P("stream", "batch", None)
    split, rows = P("batch"), P("batch", None)
    return jax.shard_map(
        functools.partial(local, batches),
        mesh=mesh,
        in_specs=(held, held) + (P(),) * 16,
        out_specs=(P(), held, held, rows, split, rows, rows, split, rows, split, split, split, rows, split, rows, split, split, split),
        check_vma=False,
    )
```
